32 devices in a mesh: grp: 2 (over y), sta: 4 (over z), band: 4 (over x, core), src: 1.
Axes of the slice: x: 2, y: 2, z: 4, core: 2. Of those that a mesh axis runs over, the one named last changes fastest.
Arguments:
- spectra: float32 [1, 192, 1024], P('src', ('grp', 'sta', 'band')), parts along dimension 1, may hold values from -6 to 6
- station_place: int32 [192], P('grp'), parts along dimension 0, may hold values from 0 to 95, each once
- tiles: int32 [32, 2], P(('grp', 'sta', 'band')), parts along dimension 0, may hold values from 0 to 1
- observed: float32 [32, 48, 48, 256], P(('grp', 'sta', 'band')), parts along dimension 0, may hold values from -8 to 8
Outputs:
- adjoint: float32 [1, 192, 1024], P('src', ('grp', 'sta', 'band')), parts along dimension 1
The draws below stay inside these ranges and needn't reach their ends.
There are 2 independent parts, one for each index of `grp`. The reference program is written for one: setup_inputs(seed, part) draws one part's arguments, and reference() takes and returns one part's arrays. A program takes and returns all parts, laid end to end along the dimension named above; each array names one. Nothing has to cross between parts.
Inputs may be any that keep to these rules, and one draw needn't show every extreme that they name: station_place is a permutation; block of station s is station_place[s] // 48.
All inputs are finite; a program needn't handle non-finite values.
Results may differ from the reference program's by a relative error of at most 0.00013.
Values sent between devices are 32-bit elements; how exact they have to be, the bound alone decides.
No kernel may reach another device: no remote copies, remote signals or barrier semaphores. Data moves between devices by JAX's collectives and lax.ppermute only.
A program may use at most 64 MiB of HBM per device.

```python
import math
import jax
import jax.numpy as jnp
from jax import lax

TILE = 48
FREQ = 512
LAGS = 256
SRC = 1
STATIONS = 96
BLOCKS = 2
TILES = 16


def touch_ends(array, own_key, smallest, largest):
    longest = array.shape.index(max(array.shape))
    spots = []
    for shift in (0, 1):
        where = [jax.random.randint(jax.random.fold_in(own_key, axis), (), 0, length) for axis, length in enumerate(array.shape)]
        where[longest] = (where[longest] + shift) % array.shape[longest]
        spots.append(tuple(where))
    return array.at[spots[0]].set(smallest).at[spots[1]].set(largest)


def levels(rng, dims, shards, least, high):
    def one(position, parts):
        steps = jax.random.uniform(jax.random.fold_in(jax.random.fold_in(rng, 6), position), (parts,), jnp.float32, least / len(shards), high / len(shards))
        return jnp.repeat(jnp.exp(steps), dims[position] // parts).reshape((-1,) + (1,) * (len(dims) - position - 1))

    gain = one(*shards[0])
    for cut in shards[1:]:
        gain = gain * one(*cut)
    return gain


def noise(stream_key, extent, scale, limit, pieces=(), held_as=jnp.bfloat16):
    drawn = scale * jax.random.normal(stream_key, extent, jnp.float32)
    if pieces:
        drawn = drawn * levels(stream_key, extent, pieces, -0.22, 0.18)
    return jnp.clip(drawn, -limit, limit).astype(held_as)


def setup_inputs(seed: int = 0, part: int = 0) -> dict:
    key_of = jax.random.split(jax.random.key(seed), 5)
    own_keys = jax.random.split(jax.random.fold_in(key_of[4], part), 5)
    spectra = noise(own_keys[0], (SRC, STATIONS, 2 * FREQ), 1.0, 6.0, ((1, 16),), jnp.float32)
    station_place = jax.random.permutation(own_keys[1], STATIONS).astype(jnp.int32)
    tiles = touch_ends(jax.random.randint(own_keys[2], (TILES, 2), 0, BLOCKS), jax.random.fold_in(own_keys[2], 1), 0, BLOCKS - 1).astype(jnp.int32)
    observed = noise(own_keys[3], (TILES, TILE, TILE, LAGS), 2.0, 8.0, ((0, 16),), jnp.float32)
    return {"spectra": spectra, "station_place": station_place, "tiles": tiles, "observed": observed}


cubic_weight = 0.1

def dft_table(freqs, lags):
    fvals = jnp.arange(freqs, dtype=jnp.float32)
    tvals = jnp.arange(lags, dtype=jnp.float32) - lags // 2
    phase = math.pi / freqs * fvals[:, None] * tvals[None, :]
    return jnp.concatenate([jnp.cos(phase), -jnp.sin(phase)], 0) * (1.0 / math.sqrt(freqs))

def cross_spectrum(left, right):
    half = left.shape[-1] // 2
    lre = left[:, :, None, :half]
    lim = left[:, :, None, half:]
    rre = right[:, None, :, :half]
    rim = right[:, None, :, half:]
    real = lax.optimization_barrier(jnp.sum(lre * rre + lim * rim, axis=0))
    imag = lax.optimization_barrier(jnp.sum(lim * rre - lre * rim, axis=0))
    return jnp.concatenate([real, imag], -1)

def adjoint_terms(spectral, left, right):
    half = left.shape[-1] // 2
    are = spectral[:, :, :half]
    aim = spectral[:, :, half:]
    hi = lax.Precision.HIGHEST
    lre, lim = (left[:, :, :half], left[:, :, half:])
    rre, rim = (right[:, :, :half], right[:, :, half:])
    row_re = jnp.einsum('pqf,sqf->spf', are, rre, precision=hi) - jnp.einsum('pqf,sqf->spf', aim, rim, precision=hi)
    row_im = jnp.einsum('pqf,sqf->spf', are, rim, precision=hi) + jnp.einsum('pqf,sqf->spf', aim, rre, precision=hi)
    col_re = jnp.einsum('pqf,spf->sqf', are, lre, precision=hi) + jnp.einsum('pqf,spf->sqf', aim, lim, precision=hi)
    col_im = jnp.einsum('pqf,spf->sqf', are, lim, precision=hi) - jnp.einsum('pqf,spf->sqf', aim, lre, precision=hi)
    rows = jnp.concatenate([row_re, row_im], -1)
    cols = jnp.concatenate([col_re, col_im], -1)
    return jnp.concatenate([rows, cols], 1)

def reference(spectra, station_place, tiles, observed):
    count = station_place.shape[0]
    tile = observed.shape[1]
    lags = observed.shape[3]
    width = spectra.shape[2]
    holder = jnp.zeros((count,), jnp.int32).at[station_place].set(jnp.arange(count, dtype=jnp.int32))
    table = dft_table(width // 2, lags)
    offsets = jnp.arange(tile, dtype=jnp.int32)

    def one_tile(items):
        pair, seen = items
        left = spectra[:, holder[pair[0] * tile + offsets]]
        right = spectra[:, holder[pair[1] * tile + offsets]]
        cross = cross_spectrum(left, right).reshape(tile * tile, width)
        lagged = jnp.dot(cross, table, precision=lax.Precision.HIGHEST, preferred_element_type=jnp.float32)
        misfit = lagged - seen.reshape(tile * tile, lags)
        weighted = misfit + cubic_weight * misfit * misfit * misfit
        spectral = jnp.dot(weighted, table.T, precision=lax.Precision.HIGHEST, preferred_element_type=jnp.float32)
        return adjoint_terms(spectral.reshape(tile, tile, width), left, right)
    terms = lax.map(one_tile, (tiles, observed))
    places = (tiles[:, :, None] * tile + offsets[None, None, :]).reshape(-1)
    targets = holder[places]
    flat = jnp.transpose(terms, (1, 0, 2, 3)).reshape(spectra.shape[0], -1, width)
    total = jnp.zeros(spectra.shape, jnp.float32).at[:, targets].add(flat)
    return total * (1.0 / tile)
```

```python
import functools
import math

import jax
import jax.numpy as jnp
from jax import lax
from jax.experimental import pallas as pl
from jax.experimental.pallas import tpu as pltpu
from jax.sharding import PartitionSpec as P

cubic_weight = 0.1
LANES = 128
bf16 = jnp.bfloat16
f32 = jnp.float32


def dft_table(freqs, lags):
    fvals = jnp.arange(freqs, dtype=jnp.float32)
    tvals = jnp.arange(lags, dtype=jnp.float32) - lags // 2
    phase = math.pi / freqs * fvals[:, None] * tvals[None, :]
    return jnp.concatenate([jnp.cos(phase), -jnp.sin(phase)], 0) * (1.0 / math.sqrt(freqs))


def split(x):
    hi = x.astype(bf16)
    return hi, (x - hi.astype(f32)).astype(bf16)


def dot(a, b):
    return jnp.dot(a, b, preferred_element_type=f32)


def table_kernel(table, th, tl, bh, bl):
    value = table[...]
    th[...], tl[...] = split(value)
    bh[...], bl[...] = split(value.T)


def split_table(table):
    size, lags = table.shape
    shapes = [(size, lags), (size, lags), (lags, size), (lags, size)]
    return pl.pallas_call(
        table_kernel,
        out_shape=[jax.ShapeDtypeStruct(s, bf16) for s in shapes],
        cost_estimate=pl.CostEstimate(
            flops=8 * size * lags, bytes_accessed=12 * size * lags, transcendentals=0
        ),
    )(table)


def bits_of(n):
    return [1 << k for k in range(n.bit_length() - 1)]


def gather_order(sta, band):
    order = [(k, 0) for k in range(sta)]
    for bit in reversed(bits_of(band)):
        order = order + [(k, b ^ bit) for k, b in order]
    return order


def scatter_order(sta, band):
    bits = bits_of(band)
    inner = [0]
    for bit in bits[1:]:
        inner = inner + [b ^ bit for b in inner]
    order = [(k, b) for k in range(sta) for b in inner]
    for bit in bits[:1]:
        order = order + [(k, b ^ bit) for k, b in order]
    return order


def pairs(n, k):
    return [(i, i ^ k) for i in range(n)]


def gather(piece, sta, band):
    got = {k: lax.ppermute(piece, "sta", pairs(sta, k)) for k in range(sta - 1, 0, -1)}
    held = [piece] + [got[k] for k in range(1, sta)]
    for bit in reversed(bits_of(band)):
        whole = jnp.concatenate(held, 0) if len(held) > 1 else held[0]
        held = [whole, lax.ppermute(whole, "band", pairs(band, bit))]
    return held


def scatter_sum(parts, sta, band):
    bits = bits_of(band)
    total = parts[0]
    if bits:
        total = total + lax.ppermute(parts[1], "band", pairs(band, bits[0]))
    if sta > 1:
        each = total.shape[0] // sta
        sent = [
            lax.ppermute(total[k * each : (k + 1) * each], "sta", pairs(sta, k))
            for k in range(sta - 1, 0, -1)
        ]
        total = total[:each]
        for part in reversed(sent):
            total = total + part
    for bit in reversed(bits[1:]):
        half = total.shape[0] // 2
        total = total[:half] + lax.ppermute(total[half:], "band", pairs(band, bit))
    return total


def station_of(offset, me, band, rows):
    return ((offset[0] ^ me[0]) * band + (offset[1] ^ me[1])) * rows


def place_stations(held, place, me, blocked, geometry):
    sta, band, rows, per = geometry
    order = gather_order(sta, band)
    here = (me[0], me[1])
    at = 0
    for ref in held:
        for n in range(ref.shape[0] // (rows * per)):
            first = station_of(order[at], here, band, rows)
            at += 1
            for r in range(rows):
                to = pl.multiple_of(place[first + r] * per, per)
                blocked[pl.ds(to, per), :] = ref[(n * rows + r) * per : (n * rows + r + 1) * per, :]


def load_block(blocked, block, out, tile, per):
    view = blocked.at[pl.ds(pl.multiple_of(block * (tile * per), tile * per), tile * per)]
    for j in range(per):
        out[:, j * LANES : (j + 1) * LANES] = view[pl.ds(j, tile, stride=per), :]


def cross_rows(p0, count, ua, ub, xh, xl, tile, half):
    for c in range(half // LANES):
        re = slice(c * LANES, (c + 1) * LANES)
        im = slice(half + c * LANES, half + (c + 1) * LANES)
        bre, bim = ub[:, re], ub[:, im]
        ares, aims = ua[pl.ds(p0, count), re], ua[pl.ds(p0, count), im]
        for p in range(count):
            at = slice(p * tile, (p + 1) * tile)
            are, aim = ares[p : p + 1], aims[p : p + 1]
            xh[at, re], xl[at, re] = split(are * bre + aim * bim)
            xh[at, im], xl[at, im] = split(aim * bre - are * bim)


def lag_rows(xh, xl, th, tl):
    return dot(xh[...], th[...]) + (dot(xl[...], th[...]) + dot(xh[...], tl[...]))


def spectral_rows(lagged, seen, bh, bl):
    misfit = lagged - seen
    weighted = misfit + cubic_weight * misfit * misfit * misfit
    wh, wl = split(weighted)
    return dot(wh, bh[...]) + (dot(wl, bh[...]) + dot(wh, bl[...]))


def adjoint_rows(p0, count, spec, ua, ub, rows, cols, tile, half):
    for c in range(half // LANES):
        re = slice(c * LANES, (c + 1) * LANES)
        im = slice(half + c * LANES, half + (c + 1) * LANES)
        bre, bim = ub[:, re], ub[:, im]
        ares, aims = ua[pl.ds(p0, count), re], ua[pl.ds(p0, count), im]
        cre, cim = cols[:, re], cols[:, im]
        rre, rim = [], []
        for p in range(count):
            at = slice(p * tile, (p + 1) * tile)
            are, aim = ares[p : p + 1], aims[p : p + 1]
            sre, sim = spec[at, re], spec[at, im]
            rre.append(jnp.sum(sre * bre - sim * bim, axis=0, keepdims=True))
            rim.append(jnp.sum(sre * bim + sim * bre, axis=0, keepdims=True))
            cre = cre + (sre * are + sim * aim)
            cim = cim + (sre * aim - sim * are)
        cols[:, re] = cre
        cols[:, im] = cim
        rows[pl.ds(p0, count), re] = jnp.concatenate(rre, 0)
        rows[pl.ds(p0, count), im] = jnp.concatenate(rim, 0)


def give_terms(tiles, place, me, rows, cols, blocked, outs, geometry, tile):
    sta, band, nrows, per = geometry
    scale = 1.0 / tile
    blocked[...] = jnp.zeros_like(blocked)
    for block, ref in ((tiles[0, 0], rows), (tiles[0, 1], cols)):
        view = blocked.at[pl.ds(pl.multiple_of(block * (tile * per), tile * per), tile * per)]
        for j in range(per):
            spot = pl.ds(j, tile, stride=per)
            view[spot, :] = view[spot, :] + ref[:, j * LANES : (j + 1) * LANES]
    order = scatter_order(sta, band)
    here = (me[0], me[1])
    at = 0
    for out in outs:
        for n in range(out.shape[0] // (nrows * per)):
            first = station_of(order[at], here, band, nrows)
            at += 1
            for r in range(nrows):
                source = pl.multiple_of(place[first + r] * per, per)
                to = (n * nrows + r) * per
                out[to : to + per, :] = blocked[pl.ds(source, per), :] * scale


def tile_kernel(
    geometry, n_held, n_out, step, forward, backward, tiles, place, me, *refs
):
    held, refs = refs[:n_held], refs[n_held:]
    tile, half = None, None
    (th, tl, bh, bl), refs = refs[:4], refs[4:]
    per = geometry[3]
    half = th.shape[0] // 2
    lags = th.shape[1]
    if backward:
        observed, refs = refs[0], refs[1:]
        if not forward:
            given, refs = refs[0], refs[1:]
        outs, refs = refs[:n_out], refs[n_out:]
    else:
        lagged_out, refs = refs[0], refs[1:]
    blocked, ua, ub, xh, xl, spec, rows, cols = refs[:8]
    tile = ua.shape[0]
    if backward:
        seen, sem = refs[8:]
        fetch = pltpu.make_async_copy(observed.at[0], seen, sem)
        fetch.start()
    place_stations(held, place, me, blocked, geometry)
    load_block(blocked, tiles[0, 0], ua, tile, per)
    load_block(blocked, tiles[0, 1], ub, tile, per)
    if backward:
        cols[...] = jnp.zeros_like(cols)
        fetch.wait()

    def body(i, carry):
        p0 = pl.multiple_of(i * step, step)
        m0 = pl.multiple_of(i * (step * tile), step * tile)
        if forward:
            cross_rows(p0, step, ua, ub, xh, xl, tile, half)
            lagged = lag_rows(xh, xl, th, tl)
        else:
            lagged = given[pl.ds(m0, step * tile), :]
        if not backward:
            lagged_out[pl.ds(m0, step * tile), :] = lagged
            return carry
        look = seen[pl.ds(p0, step)].reshape(step * tile, lags)
        spec[...] = spectral_rows(lagged, look, bh, bl)
        adjoint_rows(p0, step, spec, ua, ub, rows, cols, tile, half)
        return carry

    lax.fori_loop(0, tile // step, body, 0)
    if backward:
        give_terms(tiles, place, me, rows, cols, blocked, outs, geometry, tile)


def tile_call(geometry, tiles, place, me, held, tables, observed, lagged=None, forward=True, backward=True):
    sta, band, rows, per = geometry
    tile, lags = observed.shape[2], observed.shape[3]
    width = per * LANES
    step = 8
    count = place.shape[0]
    smem = pl.BlockSpec(memory_space=pltpu.SMEM)
    vmem = pl.BlockSpec(memory_space=pltpu.VMEM)
    anys = pl.BlockSpec(memory_space=pl.ANY)
    args = [tiles, place, me, *held, *tables]
    specs = [smem] * 3 + [vmem] * (len(held) + 4)
    n_out = 2 if band > 1 else 1
    scratch = [
        pltpu.VMEM((count * per, LANES), f32),
        pltpu.VMEM((tile, width), f32),
        pltpu.VMEM((tile, width), f32),
        pltpu.VMEM((step * tile, width), bf16),
        pltpu.VMEM((step * tile, width), bf16),
        pltpu.VMEM((step * tile, width), f32),
        pltpu.VMEM((tile, width), f32),
        pltpu.VMEM((tile, width), f32),
    ]
    if backward:
        args.append(observed)
        specs.append(anys)
        if not forward:
            args.append(lagged)
            specs.append(vmem)
        out_shape = [jax.ShapeDtypeStruct((count * per // n_out, LANES), f32)] * n_out
        scratch += [pltpu.VMEM((tile, tile, lags), f32), pltpu.SemaphoreType.DMA]
    else:
        out_shape = [jax.ShapeDtypeStruct((tile * tile, lags), f32)]
    pairs_count = tile * tile
    return pl.pallas_call(
        functools.partial(tile_kernel, geometry, len(held), n_out, step, forward, backward),
        in_specs=specs,
        out_specs=[vmem] * len(out_shape),
        out_shape=out_shape,
        scratch_shapes=scratch,
        compiler_params=pltpu.CompilerParams(vmem_limit_bytes=32 * 2**20),
        cost_estimate=pl.CostEstimate(
            flops=12 * pairs_count * width * lags, bytes_accessed=16 * pairs_count * lags, transcendentals=0
        ),
    )(*args)


def local(sizes, spectra, place, tiles, observed):
    sta, band, src = sizes
    width = spectra.shape[2]
    rows = spectra.shape[1]
    per = width // LANES
    geometry = (sta, band, rows, per)
    piece = spectra.reshape(rows * per, LANES)
    held = gather(piece, sta, band)
    me = jnp.stack([lax.axis_index("sta"), lax.axis_index("band")]).astype(jnp.int32)
    tables = split_table(dft_table(width // 2, observed.shape[3]))
    if src == 1:
        parts = tile_call(geometry, tiles, place, me, held, tables, observed)
    else:
        (lagged,) = tile_call(geometry, tiles, place, me, held, tables, observed, backward=False)
        lagged = lax.psum(lagged, "src")
        parts = tile_call(geometry, tiles, place, me, held, tables, observed, lagged, forward=False)
    return scatter_sum(parts, sta, band).reshape(spectra.shape)


def solution(mesh):
    placed = (
        P("src", ("grp", "sta", "band"), None),
        P("grp"),
        P(("grp", "sta", "band"), None),
        P(("grp", "sta", "band"), None, None, None),
    )
    sizes = tuple(mesh.shape[name] for name in ("sta", "band", "src"))
    return jax.shard_map(
        functools.partial(local, sizes),
        mesh=mesh,
        in_specs=placed,
        out_specs=P("src", ("grp", "sta", "band"), None),
        check_vma=False,
    )
```

```python
import functools
import math

import jax
import jax.numpy as jnp
import ml_dtypes
import numpy as np
from jax import lax
from jax.experimental import pallas as pl
from jax.experimental.pallas import tpu as pltpu
from jax.sharding import PartitionSpec as P

cubic_weight = 0.1
LANES = 128
bf16 = jnp.bfloat16
f32 = jnp.float32


def dft_table(freqs, lags):
    fvals = np.arange(freqs, dtype=np.float32)
    tvals = np.arange(lags, dtype=np.float32) - np.float32(lags // 2)
    phase = (np.float32(math.pi / freqs) * fvals[:, None]) * tvals[None, :]
    wave = np.exp(1j * phase.astype(np.float64))
    parts = np.concatenate([wave.real, -wave.imag], 0).astype(np.float32)
    return parts * np.float32(1.0 / math.sqrt(freqs))


def split_table(freqs, lags):
    table = dft_table(freqs, lags)
    hi = table.astype(ml_dtypes.bfloat16)
    lo = (table - hi.astype(np.float32)).astype(ml_dtypes.bfloat16)
    return [jnp.asarray(t) for t in (hi, lo, hi.T.copy(), lo.T.copy())]


def split(x):
    hi = x.astype(bf16)
    return hi, (x - hi.astype(f32)).astype(bf16)


def dot(a, b):
    return jnp.dot(a, b, preferred_element_type=f32)


def stage_kernel(*refs):
    count = len(refs) // 2
    sources, (*kept, sems) = refs[:count], refs[count:]
    copies = [pltpu.make_async_copy(s, k, sems.at[n]) for n, (s, k) in enumerate(zip(sources, kept))]
    for copy in copies:
        copy.start()
    for copy in copies:
        copy.wait()


def stage(vectors, scalars):
    arrays = list(vectors) + list(scalars)
    shapes = [pltpu.VMEM(a.shape, a.dtype) for a in vectors]
    shapes += [pltpu.SMEM(a.shape, a.dtype) for a in scalars]
    kept = pl.pallas_call(
        stage_kernel,
        in_specs=[pl.BlockSpec(memory_space=pl.ANY)] * len(arrays),
        out_specs=[pl.BlockSpec(memory_space=pltpu.VMEM)] * len(vectors)
        + [pl.BlockSpec(memory_space=pltpu.SMEM)] * len(scalars),
        out_shape=shapes,
        scratch_shapes=[pltpu.SemaphoreType.DMA((len(arrays),))],
        compiler_params=pltpu.CompilerParams(vmem_limit_bytes=58 * 2**20),
        cost_estimate=pl.CostEstimate(
            flops=0, bytes_accessed=2 * sum(a.size * a.dtype.itemsize for a in vectors), transcendentals=0
        ),
    )(*arrays)
    return kept[: len(vectors)], kept[len(vectors) :]


def bits_of(n):
    return [1 << k for k in range(n.bit_length() - 1)]


def gather_order(sta, band):
    order = [(k, 0) for k in range(sta)]
    for bit in reversed(bits_of(band)):
        order = order + [(k, b ^ bit) for k, b in order]
    return order


def scatter_order(sta, band):
    bits = bits_of(band)
    inner = [0]
    for bit in bits[1:]:
        inner = inner + [b ^ bit for b in inner]
    order = [(k, b) for k in range(sta) for b in inner]
    for bit in bits[:1]:
        order = order + [(k, b ^ bit) for k, b in order]
    return order


def pairs(n, k):
    return [(i, i ^ k) for i in range(n)]


def gather(piece, own, sta, band):
    got = {k: lax.ppermute(piece, "sta", pairs(sta, k)) for k in range(sta - 1, 0, -1)}
    held = [own] + [got[k] for k in range(1, sta)]
    for bit in reversed(bits_of(band)):
        whole = jnp.concatenate(held, 0) if len(held) > 1 else held[0]
        held = [whole, lax.ppermute(whole, "band", pairs(band, bit))]
    return held


def scatter_sum(parts, sta, band):
    bits = bits_of(band)
    total = parts[0]
    if bits:
        total = total + lax.ppermute(parts[1], "band", pairs(band, bits[0]))
    if sta > 1:
        each = total.shape[0] // sta
        sent = [
            lax.ppermute(total[k * each : (k + 1) * each], "sta", pairs(sta, k))
            for k in range(sta - 1, 0, -1)
        ]
        total = total[:each]
        for part in reversed(sent):
            total = total + part
    for bit in reversed(bits[1:]):
        half = total.shape[0] // 2
        total = total[:half] + lax.ppermute(total[half:], "band", pairs(band, bit))
    return total


def station_of(offset, me, band, rows):
    return ((offset[0] ^ me[0]) * band + (offset[1] ^ me[1])) * rows


def place_stations(held, place, me, blocked, geometry):
    sta, band, rows, per = geometry
    order = gather_order(sta, band)
    here = (me[0], me[1])
    at = 0
    for ref in held:
        for n in range(ref.shape[0] // (rows * per)):
            first = station_of(order[at], here, band, rows)
            at += 1
            for r in range(rows):
                to = pl.multiple_of(place[first + r] * per, per)
                blocked[pl.ds(to, per), :] = ref[(n * rows + r) * per : (n * rows + r + 1) * per, :]


def load_block(blocked, block, out, tile, per):
    view = blocked.at[pl.ds(pl.multiple_of(block * (tile * per), tile * per), tile * per)]
    for j in range(per):
        out[:, j * LANES : (j + 1) * LANES] = view[pl.ds(j, tile, stride=per), :]


def cross_rows(p0, count, ua, ub, xh, xl, tile, half):
    for c in range(half // LANES):
        re = slice(c * LANES, (c + 1) * LANES)
        im = slice(half + c * LANES, half + (c + 1) * LANES)
        bre, bim = ub[:, re], ub[:, im]
        ares, aims = ua[p0 : p0 + count, re], ua[p0 : p0 + count, im]
        for p in range(count):
            at = slice(p * tile, (p + 1) * tile)
            are, aim = ares[p : p + 1], aims[p : p + 1]
            xh[at, re], xl[at, re] = split(are * bre + aim * bim)
            xh[at, im], xl[at, im] = split(aim * bre - are * bim)


def lag_rows(xh, xl, th, tl):
    return dot(xh[...], th[...]) + (dot(xl[...], th[...]) + dot(xh[...], tl[...]))


def spectral_rows(wh, wl, bh, bl):
    return dot(wh, bh[...]) + (dot(wl, bh[...]) + dot(wh, bl[...]))


def adjoint_rows(p0, count, spec, ua, ub, rows, cols, tile, half):
    for c in range(half // LANES):
        re = slice(c * LANES, (c + 1) * LANES)
        im = slice(half + c * LANES, half + (c + 1) * LANES)
        bre, bim = ub[:, re], ub[:, im]
        ares, aims = ua[p0 : p0 + count, re], ua[p0 : p0 + count, im]
        cre, cim = cols[:, re], cols[:, im]
        rre, rim = [], []
        for p in range(count):
            at = slice(p * tile, (p + 1) * tile)
            are, aim = ares[p : p + 1], aims[p : p + 1]
            sre, sim = spec[at, re], spec[at, im]
            rre.append(jnp.sum(sre * bre - sim * bim, axis=0, keepdims=True))
            rim.append(jnp.sum(sre * bim + sim * bre, axis=0, keepdims=True))
            cre = cre + (sre * are + sim * aim)
            cim = cim + (sre * aim - sim * are)
        cols[:, re] = cre
        cols[:, im] = cim
        rows[p0 : p0 + count, re] = jnp.concatenate(rre, 0)
        rows[p0 : p0 + count, im] = jnp.concatenate(rim, 0)


def give_terms(tiles, place, me, rows, cols, blocked, outs, geometry, tile):
    sta, band, nrows, per = geometry
    scale = 1.0 / tile
    blocked[...] = jnp.zeros_like(blocked)
    for block, ref in ((tiles[0, 0], rows), (tiles[0, 1], cols)):
        view = blocked.at[pl.ds(pl.multiple_of(block * (tile * per), tile * per), tile * per)]
        for j in range(per):
            spot = pl.ds(j, tile, stride=per)
            view[spot, :] = view[spot, :] + ref[:, j * LANES : (j + 1) * LANES]
    order = scatter_order(sta, band)
    here = (me[0], me[1])
    at = 0
    for out in outs:
        for n in range(out.shape[0] // (nrows * per)):
            first = station_of(order[at], here, band, nrows)
            at += 1
            for r in range(nrows):
                source = pl.multiple_of(place[first + r] * per, per)
                to = (n * nrows + r) * per
                out[to : to + per, :] = blocked[pl.ds(source, per), :] * scale


def tile_kernel(
    geometry, n_held, n_out, step, forward, backward, tiles, place, me, *refs
):
    held, refs = refs[:n_held], refs[n_held:]
    tile, half = None, None
    (th, tl, bh, bl), refs = refs[:4], refs[4:]
    per = geometry[3]
    half = th.shape[0] // 2
    lags = th.shape[1]
    if backward:
        seen, refs = refs[0], refs[1:]
        if not forward:
            given, refs = refs[0], refs[1:]
        outs, refs = refs[:n_out], refs[n_out:]
    else:
        lagged_out, refs = refs[0], refs[1:]
    blocked, ua, ub, rows, cols = refs[:5]
    xh, xl, spec = refs[5:7], refs[7:9], refs[9:11]
    tile = ua.shape[0]
    if backward:
        wh, wl = refs[11:]
    place_stations(held, place, me, blocked, geometry)
    load_block(blocked, tiles[0, 0], ua, tile, per)
    load_block(blocked, tiles[0, 1], ub, tile, per)
    if backward:
        cols[...] = jnp.zeros_like(cols)

    steps = tile // step

    def cross_step(i):
        if forward and i < steps:
            cross_rows(i * step, step, ua, ub, xh[i % 2], xl[i % 2], tile, half)

    def lag_step(i):
        span = slice(i * step * tile, (i + 1) * step * tile)
        lagged = lag_rows(xh[i % 2], xl[i % 2], th, tl) if forward else given[span, :]
        if backward:
            misfit = lagged - seen[i * step : (i + 1) * step].reshape(step * tile, lags)
            weighted = misfit + cubic_weight * misfit * misfit * misfit
            wh[span, :], wl[span, :] = split(weighted)
        else:
            lagged_out[span, :] = lagged

    def spectral_step(i):
        if i < steps:
            span = slice(i * step * tile, (i + 1) * step * tile)
            spec[i % 2][...] = spectral_rows(wh[span, :], wl[span, :], bh, bl)

    cross_step(0)
    for i in range(steps):
        cross_step(i + 1)
        lag_step(i)
    if backward:
        spectral_step(0)
        for i in range(steps):
            spectral_step(i + 1)
            adjoint_rows(i * step, step, spec[i % 2], ua, ub, rows, cols, tile, half)
    if backward:
        give_terms(tiles, place, me, rows, cols, blocked, outs, geometry, tile)


def tile_call(geometry, tiles, place, me, held, tables, seen, lagged=None, forward=True, backward=True):
    sta, band, rows, per = geometry
    tile, lags = seen.shape[1:]
    width = per * LANES
    step = 16
    count = place.shape[0]
    smem = pl.BlockSpec(memory_space=pltpu.SMEM)
    vmem = pl.BlockSpec(memory_space=pltpu.VMEM)
    args = [tiles, place, me, *held, *tables]
    specs = [smem] * 3 + [vmem] * (len(held) + 4)
    n_out = 2 if band > 1 else 1
    scratch = [
        pltpu.VMEM((count * per, LANES), f32),
        pltpu.VMEM((tile, width), f32),
        pltpu.VMEM((tile, width), f32),
        pltpu.VMEM((tile, width), f32),
        pltpu.VMEM((tile, width), f32),
    ]
    scratch += [pltpu.VMEM((step * tile, width), bf16)] * 4
    scratch += [pltpu.VMEM((step * tile, width), f32)] * 2
    if backward:
        args.append(seen)
        specs.append(vmem)
        if not forward:
            args.append(lagged)
            specs.append(vmem)
        out_shape = [jax.ShapeDtypeStruct((count * per // n_out, LANES), f32)] * n_out
        scratch += [
            pltpu.VMEM((tile * tile, lags), bf16),
            pltpu.VMEM((tile * tile, lags), bf16),
        ]
    else:
        out_shape = [jax.ShapeDtypeStruct((tile * tile, lags), f32)]
    pairs_count = tile * tile
    return pl.pallas_call(
        functools.partial(tile_kernel, geometry, len(held), n_out, step, forward, backward),
        in_specs=specs,
        out_specs=[vmem] * len(out_shape),
        out_shape=out_shape,
        scratch_shapes=scratch,
        compiler_params=pltpu.CompilerParams(vmem_limit_bytes=32 * 2**20),
        cost_estimate=pl.CostEstimate(
            flops=12 * pairs_count * width * lags, bytes_accessed=16 * pairs_count * lags, transcendentals=0
        ),
    )(*args)


def local(sizes, spectra, place, tiles, observed):
    sta, band, src = sizes
    width = spectra.shape[2]
    rows = spectra.shape[1]
    per = width // LANES
    geometry = (sta, band, rows, per)
    piece = spectra.reshape(rows * per, LANES)
    me = jnp.stack([lax.axis_index("sta"), lax.axis_index("band")]).astype(jnp.int32)
    tables = split_table(width // 2, observed.shape[3])
    (own, seen, *tables), (tiles, place, me) = stage([piece, observed[0], *tables], [tiles, place, me])
    held = gather(piece, own, sta, band)
    if src == 1:
        parts = tile_call(geometry, tiles, place, me, held, tables, seen)
    else:
        (lagged,) = tile_call(geometry, tiles, place, me, held, tables, seen, backward=False)
        lagged = lax.psum(lagged, "src")
        parts = tile_call(geometry, tiles, place, me, held, tables, seen, lagged, forward=False)
    return scatter_sum(parts, sta, band).reshape(spectra.shape)


def solution(mesh):
    placed = (
        P("src", ("grp", "sta", "band"), None),
        P("grp"),
        P(("grp", "sta", "band"), None),
        P(("grp", "sta", "band"), None, None, None),
    )
    sizes = tuple(mesh.shape[name] for name in ("sta", "band", "src"))
    return jax.shard_map(
        functools.partial(local, sizes),
        mesh=mesh,
        in_specs=placed,
        out_specs=P("src", ("grp", "sta", "band"), None),
        check_vma=False,
    )
```

```python
import functools
import math

import jax
import jax.numpy as jnp
import ml_dtypes
import numpy as np
from jax import lax
from jax.experimental import pallas as pl
from jax.experimental.pallas import tpu as pltpu
from jax.sharding import PartitionSpec as P

cubic_weight = 0.1
LANES = 128
bf16 = jnp.bfloat16
f32 = jnp.float32


def dft_table(freqs, lags):
    fvals = np.arange(freqs, dtype=np.float32)
    tvals = np.arange(lags, dtype=np.float32) - np.float32(lags // 2)
    phase = (np.float32(math.pi / freqs) * fvals[:, None]) * tvals[None, :]
    wave = np.exp(1j * phase.astype(np.float64))
    parts = np.concatenate([wave.real, -wave.imag], 0).astype(np.float32)
    return parts * np.float32(1.0 / math.sqrt(freqs))


def split_table(freqs, lags):
    table = dft_table(freqs, lags)
    hi = table.astype(ml_dtypes.bfloat16)
    lo = (table - hi.astype(np.float32)).astype(ml_dtypes.bfloat16)
    return [jnp.asarray(t) for t in (hi, lo, hi.T.copy(), lo.T.copy())]


def split(x):
    hi = x.astype(bf16)
    return hi, (x - hi.astype(f32)).astype(bf16)


def dot(a, b):
    return jnp.dot(a, b, preferred_element_type=f32)


def stage_kernel(*refs):
    count = len(refs) // 2
    sources, (*kept, sems) = refs[:count], refs[count:]
    copies = [pltpu.make_async_copy(s, k, sems.at[n]) for n, (s, k) in enumerate(zip(sources, kept))]
    for copy in copies:
        copy.start()
    for copy in copies:
        copy.wait()


def stage(vectors, scalars):
    arrays = list(vectors) + list(scalars)
    shapes = [pltpu.VMEM(a.shape, a.dtype) for a in vectors]
    shapes += [pltpu.SMEM(a.shape, a.dtype) for a in scalars]
    kept = pl.pallas_call(
        stage_kernel,
        in_specs=[pl.BlockSpec(memory_space=pl.ANY)] * len(arrays),
        out_specs=[pl.BlockSpec(memory_space=pltpu.VMEM)] * len(vectors)
        + [pl.BlockSpec(memory_space=pltpu.SMEM)] * len(scalars),
        out_shape=shapes,
        scratch_shapes=[pltpu.SemaphoreType.DMA((len(arrays),))],
        compiler_params=pltpu.CompilerParams(vmem_limit_bytes=58 * 2**20),
        cost_estimate=pl.CostEstimate(
            flops=0, bytes_accessed=2 * sum(a.size * a.dtype.itemsize for a in vectors), transcendentals=0
        ),
    )(*arrays)
    return kept[: len(vectors)], kept[len(vectors) :]


def bits_of(n):
    return [1 << k for k in range(n.bit_length() - 1)]


def gather_order(sta, band):
    order = [(k, 0) for k in range(sta)]
    for bit in reversed(bits_of(band)):
        order = order + [(k, b ^ bit) for k, b in order]
    return order


def scatter_order(sta, band):
    bits = bits_of(band)
    inner = [0]
    for bit in bits[1:]:
        inner = inner + [b ^ bit for b in inner]
    order = [(k, b) for k in range(sta) for b in inner]
    for bit in bits[:1]:
        order = order + [(k, b ^ bit) for k, b in order]
    return order


def pairs(n, k):
    return [(i, i ^ k) for i in range(n)]


def gather(piece, own, sta, band):
    got = {k: lax.ppermute(piece, "sta", pairs(sta, k)) for k in range(sta - 1, 0, -1)}
    held = [jnp.concatenate([own] + [got[k] for k in range(1, sta)], 0)]
    for bit in reversed(bits_of(band)):
        held = held + [lax.ppermute(one, "band", pairs(band, bit)) for one in held]
    return held


def scatter_sum(parts, sta, band):
    bits = bits_of(band)
    total = parts[0]
    if bits:
        total = total + lax.ppermute(parts[1], "band", pairs(band, bits[0]))
    if sta > 1:
        each = total.shape[0] // sta
        sent = [
            lax.ppermute(total[k * each : (k + 1) * each], "sta", pairs(sta, k))
            for k in range(sta - 1, 0, -1)
        ]
        total = total[:each]
        for part in reversed(sent):
            total = total + part
    for bit in reversed(bits[1:]):
        half = total.shape[0] // 2
        total = total[:half] + lax.ppermute(total[half:], "band", pairs(band, bit))
    return total


def station_of(offset, me, band, rows):
    return ((offset[0] ^ me[0]) * band + (offset[1] ^ me[1])) * rows


def place_stations(held, place, me, blocked, geometry):
    sta, band, rows, per = geometry
    order = gather_order(sta, band)
    here = (me[0], me[1])
    at = 0
    for ref in held:
        for n in range(ref.shape[0] // (rows * per)):
            first = station_of(order[at], here, band, rows)
            at += 1
            for r in range(rows):
                to = pl.multiple_of(place[first + r] * per, per)
                blocked[pl.ds(to, per), :] = ref[(n * rows + r) * per : (n * rows + r + 1) * per, :]


def load_block(blocked, block, out, tile, per):
    view = blocked.at[pl.ds(pl.multiple_of(block * (tile * per), tile * per), tile * per)]
    for j in range(per):
        out[:, j * LANES : (j + 1) * LANES] = view[pl.ds(j, tile, stride=per), :]


def cross_rows(chunks, p0, count, ua, ub, xh, xl, tile, half):
    for c in chunks:
        re = slice(c * LANES, (c + 1) * LANES)
        im = slice(half + c * LANES, half + (c + 1) * LANES)
        bre, bim = ub[:, re], ub[:, im]
        ares, aims = ua[p0 : p0 + count, re], ua[p0 : p0 + count, im]
        for p in range(count):
            at = slice(p * tile, (p + 1) * tile)
            are, aim = ares[p : p + 1], aims[p : p + 1]
            xh[at, re], xl[at, re] = split(are * bre + aim * bim)
            xh[at, im], xl[at, im] = split(aim * bre - are * bim)


def lag_part(c, xh, xl, th, tl, half):
    re = slice(c * LANES, (c + 1) * LANES)
    im = slice(half + c * LANES, half + (c + 1) * LANES)
    left = [x[:, at] for x in (xh, xl, xh) for at in (re, im)]
    right = [t[at, :] for t in (th, th, tl) for at in (re, im)]
    return dot(jnp.concatenate(left, 1), jnp.concatenate(right, 0))


def spectral_part(c, chunks, wh, wl, bh, bl):
    size = bh.shape[1] // chunks
    at = slice(c * size, (c + 1) * size)
    left = jnp.concatenate([wh, wl, wh], 1)
    return at, dot(left, jnp.concatenate([bh[:, at], bh[:, at], bl[:, at]], 0))


def adjoint_rows(chunks, p0, count, spec, ua, ub, rows, cols, tile, half):
    for c in chunks:
        re = slice(c * LANES, (c + 1) * LANES)
        im = slice(half + c * LANES, half + (c + 1) * LANES)
        bre, bim = ub[:, re], ub[:, im]
        ares, aims = ua[p0 : p0 + count, re], ua[p0 : p0 + count, im]
        cre, cim = cols[:, re], cols[:, im]
        rre, rim = [], []
        for p in range(count):
            at = slice(p * tile, (p + 1) * tile)
            are, aim = ares[p : p + 1], aims[p : p + 1]
            sre, sim = spec[at, re], spec[at, im]
            rre.append(jnp.sum(sre * bre - sim * bim, axis=0, keepdims=True))
            rim.append(jnp.sum(sre * bim + sim * bre, axis=0, keepdims=True))
            cre = cre + (sre * are + sim * aim)
            cim = cim + (sre * aim - sim * are)
        cols[:, re] = cre
        cols[:, im] = cim
        rows[p0 : p0 + count, re] = jnp.concatenate(rre, 0)
        rows[p0 : p0 + count, im] = jnp.concatenate(rim, 0)


def give_terms(tiles, place, me, rows, cols, blocked, outs, geometry, tile):
    sta, band, nrows, per = geometry
    scale = 1.0 / tile
    blocked[...] = jnp.zeros_like(blocked)
    for block, ref in ((tiles[0, 0], rows), (tiles[0, 1], cols)):
        view = blocked.at[pl.ds(pl.multiple_of(block * (tile * per), tile * per), tile * per)]
        for j in range(per):
            spot = pl.ds(j, tile, stride=per)
            view[spot, :] = view[spot, :] + ref[:, j * LANES : (j + 1) * LANES]
    order = scatter_order(sta, band)
    here = (me[0], me[1])
    at = 0
    for out in outs:
        for n in range(out.shape[0] // (nrows * per)):
            first = station_of(order[at], here, band, nrows)
            at += 1
            for r in range(nrows):
                source = pl.multiple_of(place[first + r] * per, per)
                to = (n * nrows + r) * per
                out[to : to + per, :] = blocked[pl.ds(source, per), :] * scale


def tile_kernel(
    geometry, n_held, n_out, step, forward, backward, tiles, place, me, *refs
):
    held, refs = refs[:n_held], refs[n_held:]
    tile, half = None, None
    (th, tl, bh, bl), refs = refs[:4], refs[4:]
    per = geometry[3]
    half = th.shape[0] // 2
    lags = th.shape[1]
    if backward:
        seen, refs = refs[0], refs[1:]
        if not forward:
            given, refs = refs[0], refs[1:]
        outs, refs = refs[:n_out], refs[n_out:]
    else:
        lagged_out, refs = refs[0], refs[1:]
    blocked, ua, ub, rows, cols = refs[:5]
    xh, xl, spec = refs[5:7], refs[7:9], refs[9:11]
    tile = ua.shape[0]
    if backward:
        wh, wl = refs[11:]
    place_stations(held, place, me, blocked, geometry)
    load_block(blocked, tiles[0, 0], ua, tile, per)
    load_block(blocked, tiles[0, 1], ub, tile, per)
    if backward:
        cols[...] = jnp.zeros_like(cols)

    steps = tile // step
    chunks = half // LANES

    def cross_step(i, c):
        if forward and i < steps:
            cross_rows(c, i * step, step, ua, ub, xh[i % 2], xl[i % 2], tile, half)

    def weigh_step(i, lagged):
        span = slice(i * step * tile, (i + 1) * step * tile)
        if backward:
            misfit = lagged - seen[i * step : (i + 1) * step].reshape(step * tile, lags)
            weighted = misfit + cubic_weight * misfit * misfit * misfit
            wh[span, :], wl[span, :] = split(weighted)
        else:
            lagged_out[span, :] = lagged

    def spectral_step(i, c):
        if i < steps:
            span = slice(i * step * tile, (i + 1) * step * tile)
            at, value = spectral_part(c, chunks, wh[span, :], wl[span, :], bh, bl)
            spec[i % 2][:, at] = value

    cross_step(0, range(chunks))
    for i in range(steps):
        if forward:
            lagged = None
            for c in range(chunks):
                part = lag_part(c, xh[i % 2], xl[i % 2], th, tl, half)
                lagged = part if lagged is None else lagged + part
                cross_step(i + 1, [c])
        else:
            lagged = given[i * step * tile : (i + 1) * step * tile, :]
        weigh_step(i, lagged)
    if backward:
        for c in range(chunks):
            spectral_step(0, c)
        for i in range(steps):
            for c in range(chunks):
                spectral_step(i + 1, c)
                adjoint_rows([c], i * step, step, spec[i % 2], ua, ub, rows, cols, tile, half)
    if backward:
        give_terms(tiles, place, me, rows, cols, blocked, outs, geometry, tile)


def tile_call(geometry, tiles, place, me, held, tables, seen, lagged=None, forward=True, backward=True):
    sta, band, rows, per = geometry
    tile, lags = seen.shape[1:]
    width = per * LANES
    step = 16
    count = place.shape[0]
    smem = pl.BlockSpec(memory_space=pltpu.SMEM)
    vmem = pl.BlockSpec(memory_space=pltpu.VMEM)
    args = [tiles, place, me, *held, *tables]
    specs = [smem] * 3 + [vmem] * (len(held) + 4)
    n_out = 2 if band > 1 else 1
    scratch = [
        pltpu.VMEM((count * per, LANES), f32),
        pltpu.VMEM((tile, width), f32),
        pltpu.VMEM((tile, width), f32),
        pltpu.VMEM((tile, width), f32),
        pltpu.VMEM((tile, width), f32),
    ]
    scratch += [pltpu.VMEM((step * tile, width), bf16)] * 4
    scratch += [pltpu.VMEM((step * tile, width), f32)] * 2
    if backward:
        args.append(seen)
        specs.append(vmem)
        if not forward:
            args.append(lagged)
            specs.append(vmem)
        out_shape = [jax.ShapeDtypeStruct((count * per // n_out, LANES), f32)] * n_out
        scratch += [
            pltpu.VMEM((tile * tile, lags), bf16),
            pltpu.VMEM((tile * tile, lags), bf16),
        ]
    else:
        out_shape = [jax.ShapeDtypeStruct((tile * tile, lags), f32)]
    pairs_count = tile * tile
    return pl.pallas_call(
        functools.partial(tile_kernel, geometry, len(held), n_out, step, forward, backward),
        in_specs=specs,
        out_specs=[vmem] * len(out_shape),
        out_shape=out_shape,
        scratch_shapes=scratch,
        compiler_params=pltpu.CompilerParams(vmem_limit_bytes=32 * 2**20),
        cost_estimate=pl.CostEstimate(
            flops=12 * pairs_count * width * lags, bytes_accessed=16 * pairs_count * lags, transcendentals=0
        ),
    )(*args)


def local(sizes, spectra, place, tiles, observed):
    sta, band, src = sizes
    width = spectra.shape[2]
    rows = spectra.shape[1]
    per = width // LANES
    geometry = (sta, band, rows, per)
    piece = spectra.reshape(rows * per, LANES)
    me = jnp.stack([lax.axis_index("sta"), lax.axis_index("band")]).astype(jnp.int32)
    tables = split_table(width // 2, observed.shape[3])
    (own, seen, *tables), (tiles, place, me) = stage([piece, observed[0], *tables], [tiles, place, me])
    held = gather(piece, own, sta, band)
    if src == 1:
        parts = tile_call(geometry, tiles, place, me, held, tables, seen)
    else:
        (lagged,) = tile_call(geometry, tiles, place, me, held, tables, seen, backward=False)
        lagged = lax.psum(lagged, "src")
        parts = tile_call(geometry, tiles, place, me, held, tables, seen, lagged, forward=False)
    return scatter_sum(parts, sta, band).reshape(spectra.shape)


def solution(mesh):
    placed = (
        P("src", ("grp", "sta", "band"), None),
        P("grp"),
        P(("grp", "sta", "band"), None),
        P(("grp", "sta", "band"), None, None, None),
    )
    sizes = tuple(mesh.shape[name] for name in ("sta", "band", "src"))
    return jax.shard_map(
        functools.partial(local, sizes),
        mesh=mesh,
        in_specs=placed,
        out_specs=P("src", ("grp", "sta", "band"), None),
        check_vma=False,
    )
```

```python
import functools
import math

import jax
import jax.numpy as jnp
import ml_dtypes
import numpy as np
from jax import lax
from jax.experimental import pallas as pl
from jax.experimental.pallas import tpu as pltpu
from jax.sharding import PartitionSpec as P

cubic_weight = 0.1
LANES = 128
bf16 = jnp.bfloat16
f32 = jnp.float32


def dft_table(freqs, lags):
    fvals = np.arange(freqs, dtype=np.float32)
    tvals = np.arange(lags, dtype=np.float32) - np.float32(lags // 2)
    phase = (np.float32(math.pi / freqs) * fvals[:, None]) * tvals[None, :]
    wave = np.exp(1j * phase.astype(np.float64))
    parts = np.concatenate([wave.real, -wave.imag], 0).astype(np.float32)
    return parts * np.float32(1.0 / math.sqrt(freqs))


def halves(table):
    hi = table.astype(ml_dtypes.bfloat16)
    return hi, (table - hi.astype(np.float32)).astype(ml_dtypes.bfloat16)


def turned(lags):
    return np.concatenate([[0], np.arange(lags // 2 - 1, 0, -1)])


def split_table(freqs, lags):
    table = dft_table(freqs, lags)
    mid = lags // 2
    th, tl = halves(table[:, np.concatenate([np.arange(mid, lags), turned(lags)])])
    even, odd = table[:freqs, mid:].T, table[freqs:, mid:].T.copy()
    odd[0] = table[freqs:, 0]
    ch, cl = halves(even)
    sh, sl = halves(odd)
    eh, el = halves(table[:freqs, 0])
    rest = np.zeros((mid, freqs), ml_dtypes.bfloat16)
    rest[0], rest[1], rest[2] = eh, eh, el
    back = [np.concatenate([ch, ch, cl, rest], 0), np.concatenate([sh, sh, sl], 0)]
    move = np.zeros((mid, mid), ml_dtypes.bfloat16)
    move[turned(lags), np.arange(mid)] = 1
    return [jnp.asarray(t) for t in (th, tl, *back, np.concatenate([move] * 3, 0))]


def split(x):
    hi = x.astype(bf16)
    return hi, (x - hi.astype(f32)).astype(bf16)


def dot(a, b):
    return jnp.dot(a, b, preferred_element_type=f32)


def stage_kernel(*refs):
    count = len(refs) // 2
    sources, (*kept, sems) = refs[:count], refs[count:]
    copies = [pltpu.make_async_copy(s, k, sems.at[n]) for n, (s, k) in enumerate(zip(sources, kept))]
    for copy in copies:
        copy.start()
    for copy in copies:
        copy.wait()


def stage(vectors, scalars):
    arrays = list(vectors) + list(scalars)
    shapes = [pltpu.VMEM(a.shape, a.dtype) for a in vectors]
    shapes += [pltpu.SMEM(a.shape, a.dtype) for a in scalars]
    kept = pl.pallas_call(
        stage_kernel,
        in_specs=[pl.BlockSpec(memory_space=pl.ANY)] * len(arrays),
        out_specs=[pl.BlockSpec(memory_space=pltpu.VMEM)] * len(vectors)
        + [pl.BlockSpec(memory_space=pltpu.SMEM)] * len(scalars),
        out_shape=shapes,
        scratch_shapes=[pltpu.SemaphoreType.DMA((len(arrays),))],
        compiler_params=pltpu.CompilerParams(vmem_limit_bytes=58 * 2**20),
        cost_estimate=pl.CostEstimate(
            flops=0, bytes_accessed=2 * sum(a.size * a.dtype.itemsize for a in vectors), transcendentals=0
        ),
    )(*arrays)
    return kept[: len(vectors)], kept[len(vectors) :]


def turn_kernel(seen, move, after, out):
    rows, pairs_in, lags = seen.shape
    mid = lags // 2
    out[:, :, :mid] = seen[:, :, mid:]
    count = 8
    for p in range(0, rows, count):
        low = seen[p : p + count, :, :mid].reshape(count * pairs_in, mid)
        high, rest = low.astype(bf16), low - low.astype(bf16).astype(f32)
        parts = jnp.concatenate([high, *split(rest)], 1)
        out[p : p + count, :, mid:] = dot(parts, move[...]).reshape(count, pairs_in, mid)


def turn(seen, move, after):
    vmem = pl.BlockSpec(memory_space=pltpu.VMEM)
    return pl.pallas_call(
        turn_kernel,
        in_specs=[vmem, vmem, pl.BlockSpec(memory_space=pl.ANY)],
        out_specs=vmem,
        out_shape=pltpu.VMEM(seen.shape, seen.dtype),
        compiler_params=pltpu.CompilerParams(vmem_limit_bytes=32 * 2**20),
        cost_estimate=pl.CostEstimate(
            flops=3 * seen.size * seen.shape[2], bytes_accessed=8 * seen.size, transcendentals=0
        ),
    )(seen, move, after)


def bits_of(n):
    return [1 << k for k in range(n.bit_length() - 1)]


def gather_order(sta, band):
    order = [(k, 0) for k in range(sta)]
    for bit in reversed(bits_of(band)):
        order = order + [(k, b ^ bit) for k, b in order]
    return order


def scatter_order(sta, band):
    bits = bits_of(band)
    inner = [0]
    for bit in bits[1:]:
        inner = inner + [b ^ bit for b in inner]
    order = [(k, b) for k in range(sta) for b in inner]
    for bit in bits[:1]:
        order = order + [(k, b ^ bit) for k, b in order]
    return order


def pairs(n, k):
    return [(i, i ^ k) for i in range(n)]


def gather(piece, own, sta, band):
    got = {k: lax.ppermute(piece, "sta", pairs(sta, k)) for k in range(sta - 1, 0, -1)}
    held = [jnp.concatenate([own] + [got[k] for k in range(1, sta)], 0)]
    for bit in reversed(bits_of(band)):
        held = held + [lax.ppermute(one, "band", pairs(band, bit)) for one in held]
    return held


def scatter_sum(parts, sta, band):
    bits = bits_of(band)
    total = parts[0]
    if bits:
        total = total + lax.ppermute(parts[1], "band", pairs(band, bits[0]))
    if sta > 1:
        each = total.shape[0] // sta
        sent = [
            lax.ppermute(total[k * each : (k + 1) * each], "sta", pairs(sta, k))
            for k in range(sta - 1, 0, -1)
        ]
        total = total[:each]
        for part in reversed(sent):
            total = total + part
    for bit in reversed(bits[1:]):
        half = total.shape[0] // 2
        total = total[:half] + lax.ppermute(total[half:], "band", pairs(band, bit))
    return total


def station_of(offset, me, band, rows):
    return ((offset[0] ^ me[0]) * band + (offset[1] ^ me[1])) * rows


def place_stations(held, place, me, blocked, geometry):
    sta, band, rows, per = geometry
    order = gather_order(sta, band)
    here = (me[0], me[1])
    at = 0
    for ref in held:
        for n in range(ref.shape[0] // (rows * per)):
            first = station_of(order[at], here, band, rows)
            at += 1
            for r in range(rows):
                to = pl.multiple_of(place[first + r] * per, per)
                blocked[pl.ds(to, per), :] = ref[(n * rows + r) * per : (n * rows + r + 1) * per, :]


def load_block(blocked, block, out, tile, per):
    view = blocked.at[pl.ds(pl.multiple_of(block * (tile * per), tile * per), tile * per)]
    for j in range(per):
        out[:, j * LANES : (j + 1) * LANES] = view[pl.ds(j, tile, stride=per), :]


def cross_rows(chunks, p0, count, ua, ub, xh, xl, tile, half):
    for c in chunks:
        re = slice(c * LANES, (c + 1) * LANES)
        im = slice(half + c * LANES, half + (c + 1) * LANES)
        bre, bim = ub[:, re], ub[:, im]
        ares, aims = ua[p0 : p0 + count, re], ua[p0 : p0 + count, im]
        for p in range(count):
            at = slice(p * tile, (p + 1) * tile)
            are, aim = ares[p : p + 1], aims[p : p + 1]
            xh[at, re], xl[at, re] = split(are * bre + aim * bim)
            xh[at, im], xl[at, im] = split(aim * bre - are * bim)


def lag_part(c, xh, xl, th, tl, half):
    re = slice(c * LANES, (c + 1) * LANES)
    im = slice(half + c * LANES, half + (c + 1) * LANES)
    left = [x[:, at] for x in (xh, xl, xh) for at in (re, im)]
    right = [t[at, :] for t in (th, th, tl) for at in (re, im)]
    return dot(jnp.concatenate(left, 1), jnp.concatenate(right, 0))


def fold(weighted, mid):
    up, down = weighted[:, :mid], weighted[:, mid:]
    column = lax.broadcasted_iota(jnp.int32, up.shape, 1)
    even = jnp.where(column == 0, up, up + down)
    odd = jnp.where(column == 0, down, up - down)
    lone = jnp.broadcast_to(down[:, :1], down.shape)
    high = lone.astype(bf16).astype(f32)
    lone = jnp.where(column == 1, lone - high, high).astype(bf16)
    return (*split(even), lone, *split(odd))


def spectral_part(c, chunks, folded, span, bc, bs, mid):
    size = 2 * LANES
    eh, el, lone, oh, ol = [folded[span, k * mid : (k + 1) * mid] for k in range(5)]
    if c < chunks // 2:
        left, right, here = [eh, el, eh, lone], bc, c
    else:
        left, right, here = [oh, ol, oh], bs, c - chunks // 2
    value = dot(jnp.concatenate(left, 1), right[:, here * size : (here + 1) * size])
    return slice(c * size, (c + 1) * size), value


def adjoint_rows(chunks, p0, count, spec, ua, ub, rows, cols, tile, half):
    for c in chunks:
        re = slice(c * LANES, (c + 1) * LANES)
        im = slice(half + c * LANES, half + (c + 1) * LANES)
        bre, bim = ub[:, re], ub[:, im]
        ares, aims = ua[p0 : p0 + count, re], ua[p0 : p0 + count, im]
        cre, cim = cols[:, re], cols[:, im]
        rre, rim = [], []
        for p in range(count):
            at = slice(p * tile, (p + 1) * tile)
            are, aim = ares[p : p + 1], aims[p : p + 1]
            sre, sim = spec[at, re], spec[at, im]
            rre.append(jnp.sum(sre * bre - sim * bim, axis=0, keepdims=True))
            rim.append(jnp.sum(sre * bim + sim * bre, axis=0, keepdims=True))
            cre = cre + (sre * are + sim * aim)
            cim = cim + (sre * aim - sim * are)
        cols[:, re] = cre
        cols[:, im] = cim
        rows[p0 : p0 + count, re] = jnp.concatenate(rre, 0)
        rows[p0 : p0 + count, im] = jnp.concatenate(rim, 0)


def give_terms(tiles, place, me, rows, cols, blocked, outs, geometry, tile):
    sta, band, nrows, per = geometry
    scale = 1.0 / tile
    blocked[...] = jnp.zeros_like(blocked)
    for block, ref in ((tiles[0, 0], rows), (tiles[0, 1], cols)):
        view = blocked.at[pl.ds(pl.multiple_of(block * (tile * per), tile * per), tile * per)]
        for j in range(per):
            spot = pl.ds(j, tile, stride=per)
            view[spot, :] = view[spot, :] + ref[:, j * LANES : (j + 1) * LANES]
    order = scatter_order(sta, band)
    here = (me[0], me[1])
    at = 0
    for out in outs:
        for n in range(out.shape[0] // (nrows * per)):
            first = station_of(order[at], here, band, nrows)
            at += 1
            for r in range(nrows):
                source = pl.multiple_of(place[first + r] * per, per)
                to = (n * nrows + r) * per
                out[to : to + per, :] = blocked[pl.ds(source, per), :] * scale


def tile_kernel(
    geometry, n_held, n_out, step, forward, backward, tiles, place, me, *refs
):
    held, refs = refs[:n_held], refs[n_held:]
    tile, half = None, None
    (th, tl, bc, bs), refs = refs[:4], refs[4:]
    per = geometry[3]
    half = th.shape[0] // 2
    lags = th.shape[1]
    if backward:
        seen, refs = refs[0], refs[1:]
        if not forward:
            given, refs = refs[0], refs[1:]
        outs, refs = refs[:n_out], refs[n_out:]
    else:
        lagged_out, refs = refs[0], refs[1:]
    blocked, ua, ub, rows, cols = refs[:5]
    xh, xl, spec = refs[5:7], refs[7:9], refs[9:11]
    tile = ua.shape[0]
    if backward:
        (folded,) = refs[11:]
    place_stations(held, place, me, blocked, geometry)
    load_block(blocked, tiles[0, 0], ua, tile, per)
    load_block(blocked, tiles[0, 1], ub, tile, per)
    if backward:
        cols[...] = jnp.zeros_like(cols)

    steps = tile // step
    chunks = half // LANES

    def cross_step(i, c):
        if forward and i < steps:
            cross_rows(c, i * step, step, ua, ub, xh[i % 2], xl[i % 2], tile, half)

    def weigh_step(i, lagged):
        span = slice(i * step * tile, (i + 1) * step * tile)
        if backward:
            misfit = lagged - seen[i * step : (i + 1) * step].reshape(step * tile, lags)
            weighted = misfit + cubic_weight * misfit * misfit * misfit
            folded[span, :] = jnp.concatenate(fold(weighted, lags // 2), 1)
        else:
            lagged_out[span, :] = lagged

    def spectral_step(i, c):
        if i < steps:
            span = slice(i * step * tile, (i + 1) * step * tile)
            at, value = spectral_part(c, chunks, folded, span, bc, bs, lags // 2)
            spec[i % 2][:, at] = value

    cross_step(0, range(chunks))
    for i in range(steps):
        if forward:
            lagged = None
            for c in range(chunks):
                part = lag_part(c, xh[i % 2], xl[i % 2], th, tl, half)
                lagged = part if lagged is None else lagged + part
                cross_step(i + 1, [c])
        else:
            lagged = given[i * step * tile : (i + 1) * step * tile, :]
        weigh_step(i, lagged)
    if backward:
        for c in range(chunks):
            spectral_step(0, c)
        for i in range(steps):
            for c in range(chunks):
                spectral_step(i + 1, c)
                adjoint_rows([c], i * step, step, spec[i % 2], ua, ub, rows, cols, tile, half)
    if backward:
        give_terms(tiles, place, me, rows, cols, blocked, outs, geometry, tile)


def tile_call(geometry, tiles, place, me, held, tables, seen, lagged=None, forward=True, backward=True):
    sta, band, rows, per = geometry
    tile, lags = seen.shape[1:]
    width = per * LANES
    step = 16
    count = place.shape[0]
    smem = pl.BlockSpec(memory_space=pltpu.SMEM)
    vmem = pl.BlockSpec(memory_space=pltpu.VMEM)
    args = [tiles, place, me, *held, *tables]
    specs = [smem] * 3 + [vmem] * (len(held) + 4)
    n_out = 2 if band > 1 else 1
    scratch = [
        pltpu.VMEM((count * per, LANES), f32),
        pltpu.VMEM((tile, width), f32),
        pltpu.VMEM((tile, width), f32),
        pltpu.VMEM((tile, width), f32),
        pltpu.VMEM((tile, width), f32),
    ]
    scratch += [pltpu.VMEM((step * tile, width), bf16)] * 4
    scratch += [pltpu.VMEM((step * tile, width), f32)] * 2
    if backward:
        args.append(seen)
        specs.append(vmem)
        if not forward:
            args.append(lagged)
            specs.append(vmem)
        out_shape = [jax.ShapeDtypeStruct((count * per // n_out, LANES), f32)] * n_out
        scratch += [
            pltpu.VMEM((tile * tile, 5 * (lags // 2)), bf16),
        ]
    else:
        out_shape = [jax.ShapeDtypeStruct((tile * tile, lags), f32)]
    pairs_count = tile * tile
    return pl.pallas_call(
        functools.partial(tile_kernel, geometry, len(held), n_out, step, forward, backward),
        in_specs=specs,
        out_specs=[vmem] * len(out_shape),
        out_shape=out_shape,
        scratch_shapes=scratch,
        compiler_params=pltpu.CompilerParams(vmem_limit_bytes=32 * 2**20),
        cost_estimate=pl.CostEstimate(
            flops=12 * pairs_count * width * lags, bytes_accessed=16 * pairs_count * lags, transcendentals=0
        ),
    )(*args)


def local(sizes, spectra, place, tiles, observed):
    sta, band, src = sizes
    width = spectra.shape[2]
    rows = spectra.shape[1]
    per = width // LANES
    geometry = (sta, band, rows, per)
    piece = spectra.reshape(rows * per, LANES)
    me = jnp.stack([lax.axis_index("sta"), lax.axis_index("band")]).astype(jnp.int32)
    tables = split_table(width // 2, observed.shape[3])
    (own, seen, *tables), (tiles, place, me) = stage([piece, observed[0], *tables], [tiles, place, me])
    held = gather(piece, own, sta, band)
    *tables, move = tables
    seen = turn(seen, move, held[0])
    if src == 1:
        parts = tile_call(geometry, tiles, place, me, held, tables, seen)
    else:
        (lagged,) = tile_call(geometry, tiles, place, me, held, tables, seen, backward=False)
        lagged = lax.psum(lagged, "src")
        parts = tile_call(geometry, tiles, place, me, held, tables, seen, lagged, forward=False)
    return scatter_sum(parts, sta, band).reshape(spectra.shape)


def solution(mesh):
    placed = (
        P("src", ("grp", "sta", "band"), None),
        P("grp"),
        P(("grp", "sta", "band"), None),
        P(("grp", "sta", "band"), None, None, None),
    )
    sizes = tuple(mesh.shape[name] for name in ("sta", "band", "src"))
    return jax.shard_map(
        functools.partial(local, sizes),
        mesh=mesh,
        in_specs=placed,
        out_specs=P("src", ("grp", "sta", "band"), None),
        check_vma=False,
    )
```

```python
import functools
import math

import jax
import jax.numpy as jnp
import ml_dtypes
import numpy as np
from jax import lax
from jax.experimental import pallas as pl
from jax.experimental.pallas import tpu as pltpu
from jax.sharding import PartitionSpec as P

cubic_weight = 0.1
LANES = 128
bf16 = jnp.bfloat16
f32 = jnp.float32


def dft_table(freqs, lags):
    fvals = np.arange(freqs, dtype=np.float32)
    tvals = np.arange(lags, dtype=np.float32) - np.float32(lags // 2)
    phase = (np.float32(math.pi / freqs) * fvals[:, None]) * tvals[None, :]
    wave = np.exp(1j * phase.astype(np.float64))
    parts = np.concatenate([wave.real, -wave.imag], 0).astype(np.float32)
    return parts * np.float32(1.0 / math.sqrt(freqs))


def halves(table):
    hi = table.astype(ml_dtypes.bfloat16)
    return hi, (table - hi.astype(np.float32)).astype(ml_dtypes.bfloat16)


def turned(lags):
    return np.concatenate([[0], np.arange(lags // 2 - 1, 0, -1)])


def split_table(freqs, lags):
    table = dft_table(freqs, lags)
    mid = lags // 2
    th, tl = halves(table[:, np.concatenate([np.arange(mid, lags), turned(lags)])])
    even, odd = table[:freqs, mid:].T, table[freqs:, mid:].T.copy()
    odd[0] = table[freqs:, 0]
    ch, cl = halves(even)
    sh, sl = halves(odd)
    eh, el = halves(table[:freqs, 0])
    rest = np.zeros((mid, freqs), ml_dtypes.bfloat16)
    rest[0], rest[1], rest[2] = eh, eh, el
    back = [np.concatenate([ch, ch, cl, rest], 0), np.concatenate([sh, sh, sl], 0)]
    move = np.zeros((mid, mid), ml_dtypes.bfloat16)
    move[turned(lags), np.arange(mid)] = 1
    return [jnp.asarray(t) for t in (th, tl, *back, np.concatenate([move] * 3, 0))]


def split(x):
    hi = x.astype(bf16)
    return hi, (x - hi.astype(f32)).astype(bf16)


def dot(a, b):
    return jnp.dot(a, b, preferred_element_type=f32)


def stage_kernel(*refs):
    count = len(refs) // 2
    sources, (*kept, sems) = refs[:count], refs[count:]
    copies = [pltpu.make_async_copy(s, k, sems.at[n]) for n, (s, k) in enumerate(zip(sources, kept))]
    for copy in copies:
        copy.start()
    for copy in copies:
        copy.wait()


def stage(vectors, scalars):
    arrays = list(vectors) + list(scalars)
    shapes = [pltpu.VMEM(a.shape, a.dtype) for a in vectors]
    shapes += [pltpu.SMEM(a.shape, a.dtype) for a in scalars]
    kept = pl.pallas_call(
        stage_kernel,
        in_specs=[pl.BlockSpec(memory_space=pl.ANY)] * len(arrays),
        out_specs=[pl.BlockSpec(memory_space=pltpu.VMEM)] * len(vectors)
        + [pl.BlockSpec(memory_space=pltpu.SMEM)] * len(scalars),
        out_shape=shapes,
        scratch_shapes=[pltpu.SemaphoreType.DMA((len(arrays),))],
        compiler_params=pltpu.CompilerParams(vmem_limit_bytes=58 * 2**20),
        cost_estimate=pl.CostEstimate(
            flops=0, bytes_accessed=2 * sum(a.size * a.dtype.itemsize for a in vectors), transcendentals=0
        ),
    )(*arrays)
    return kept[: len(vectors)], kept[len(vectors) :]


def turn_kernel(seen, move, after, out):
    rows, pairs_in, lags = seen.shape
    mid = lags // 2
    out[:, :, :mid] = seen[:, :, mid:]
    count = 8
    for p in range(0, rows, count):
        low = seen[p : p + count, :, :mid].reshape(count * pairs_in, mid)
        high, rest = low.astype(bf16), low - low.astype(bf16).astype(f32)
        parts = jnp.concatenate([high, *split(rest)], 1)
        out[p : p + count, :, mid:] = dot(parts, move[...]).reshape(count, pairs_in, mid)


def turn(seen, move, after):
    vmem = pl.BlockSpec(memory_space=pltpu.VMEM)
    return pl.pallas_call(
        turn_kernel,
        in_specs=[vmem, vmem, pl.BlockSpec(memory_space=pl.ANY)],
        out_specs=vmem,
        out_shape=pltpu.VMEM(seen.shape, seen.dtype),
        compiler_params=pltpu.CompilerParams(vmem_limit_bytes=32 * 2**20),
        cost_estimate=pl.CostEstimate(
            flops=3 * seen.size * seen.shape[2], bytes_accessed=8 * seen.size, transcendentals=0
        ),
    )(seen, move, after)


def bits_of(n):
    return [1 << k for k in range(n.bit_length() - 1)]


def gather_order(sta, band):
    order = [(k, 0) for k in range(sta)]
    for bit in reversed(bits_of(band)):
        order = order + [(k, b ^ bit) for k, b in order]
    return order


def scatter_order(sta, band):
    bits = bits_of(band)
    inner = [0]
    for bit in bits[1:]:
        inner = inner + [b ^ bit for b in inner]
    order = [(k, b) for k in range(sta) for b in inner]
    for bit in bits[:1]:
        order = order + [(k, b ^ bit) for k, b in order]
    return order


def pairs(n, k):
    return [(i, i ^ k) for i in range(n)]


def gather(piece, own, sta, band):
    got = {k: lax.ppermute(piece, "sta", pairs(sta, k)) for k in range(sta - 1, 0, -1)}
    held = [jnp.concatenate([own] + [got[k] for k in range(1, sta)], 0)]
    for bit in reversed(bits_of(band)):
        held = held + [lax.ppermute(one, "band", pairs(band, bit)) for one in held]
    return held


def scatter_sum(parts, sta, band):
    bits = bits_of(band)
    total = parts[0]
    if bits:
        total = total + lax.ppermute(parts[1], "band", pairs(band, bits[0]))
    if sta > 1:
        each = total.shape[0] // sta
        sent = [
            lax.ppermute(total[k * each : (k + 1) * each], "sta", pairs(sta, k))
            for k in range(sta - 1, 0, -1)
        ]
        total = total[:each]
        for part in reversed(sent):
            total = total + part
    for bit in reversed(bits[1:]):
        half = total.shape[0] // 2
        total = total[:half] + lax.ppermute(total[half:], "band", pairs(band, bit))
    return total


def station_of(offset, me, band, rows):
    return ((offset[0] ^ me[0]) * band + (offset[1] ^ me[1])) * rows


def place_stations(held, place, blocked, geometry):
    sta, band, rows, per = geometry
    order = gather_order(sta, band)
    here = (lax.axis_index("sta"), lax.axis_index("band"))
    at = 0
    for ref in held:
        for n in range(ref.shape[0] // (rows * per)):
            first = station_of(order[at], here, band, rows)
            at += 1
            for r in range(rows):
                to = pl.multiple_of(place[first + r] * per, per)
                blocked[pl.ds(to, per), :] = ref[(n * rows + r) * per : (n * rows + r + 1) * per, :]


def load_block(blocked, block, out, tile, per):
    view = blocked.at[pl.ds(pl.multiple_of(block * (tile * per), tile * per), tile * per)]
    for j in range(per):
        out[:, j * LANES : (j + 1) * LANES] = view[pl.ds(j, tile, stride=per), :]


def cross_rows(chunks, p0, count, ua, ub, xh, xl, tile, half):
    for c in chunks:
        re = slice(c * LANES, (c + 1) * LANES)
        im = slice(half + c * LANES, half + (c + 1) * LANES)
        bre, bim = ub[:, re], ub[:, im]
        ares, aims = ua[p0 : p0 + count, re], ua[p0 : p0 + count, im]
        for p in range(count):
            at = slice(p * tile, (p + 1) * tile)
            are, aim = ares[p : p + 1], aims[p : p + 1]
            xh[at, re], xl[at, re] = split(are * bre + aim * bim)
            xh[at, im], xl[at, im] = split(aim * bre - are * bim)


def lag_part(c, xh, xl, th, tl, half):
    re = slice(c * LANES, (c + 1) * LANES)
    im = slice(half + c * LANES, half + (c + 1) * LANES)
    left = [x[:, at] for x in (xh, xl, xh) for at in (re, im)]
    right = [t[at, :] for t in (th, th, tl) for at in (re, im)]
    return dot(jnp.concatenate(left, 1), jnp.concatenate(right, 0))


def fold(weighted, mid):
    up, down = weighted[:, :mid], weighted[:, mid:]
    column = lax.broadcasted_iota(jnp.int32, up.shape, 1)
    even = jnp.where(column == 0, up, up + down)
    odd = jnp.where(column == 0, down, up - down)
    lone = jnp.broadcast_to(down[:, :1], down.shape)
    high = lone.astype(bf16).astype(f32)
    lone = jnp.where(column == 1, lone - high, high).astype(bf16)
    return (*split(even), lone, *split(odd))


def spectral_part(c, chunks, folded, span, bc, bs, mid):
    size = 2 * LANES
    eh, el, lone, oh, ol = [folded[span, k * mid : (k + 1) * mid] for k in range(5)]
    if c < chunks // 2:
        left, right, here = [eh, el, eh, lone], bc, c
    else:
        left, right, here = [oh, ol, oh], bs, c - chunks // 2
    value = dot(jnp.concatenate(left, 1), right[:, here * size : (here + 1) * size])
    return slice(c * size, (c + 1) * size), value


def adjoint_rows(chunks, p0, count, spec, ua, ub, rows, cols, tile, half):
    for c in chunks:
        re = slice(c * LANES, (c + 1) * LANES)
        im = slice(half + c * LANES, half + (c + 1) * LANES)
        bre, bim = ub[:, re], ub[:, im]
        ares, aims = ua[p0 : p0 + count, re], ua[p0 : p0 + count, im]
        cre, cim = cols[:, re], cols[:, im]
        rre, rim = [], []
        for p in range(count):
            at = slice(p * tile, (p + 1) * tile)
            are, aim = ares[p : p + 1], aims[p : p + 1]
            sre, sim = spec[at, re], spec[at, im]
            rre.append(jnp.sum(sre * bre - sim * bim, axis=0, keepdims=True))
            rim.append(jnp.sum(sre * bim + sim * bre, axis=0, keepdims=True))
            cre = cre + (sre * are + sim * aim)
            cim = cim + (sre * aim - sim * are)
        cols[:, re] = cre
        cols[:, im] = cim
        rows[p0 : p0 + count, re] = jnp.concatenate(rre, 0)
        rows[p0 : p0 + count, im] = jnp.concatenate(rim, 0)


def give_terms(tiles, place, rows, cols, blocked, outs, geometry, tile):
    sta, band, nrows, per = geometry
    scale = 1.0 / tile
    blocked[...] = jnp.zeros_like(blocked)
    for block, ref in ((tiles[0, 0], rows), (tiles[0, 1], cols)):
        view = blocked.at[pl.ds(pl.multiple_of(block * (tile * per), tile * per), tile * per)]
        for j in range(per):
            spot = pl.ds(j, tile, stride=per)
            view[spot, :] = view[spot, :] + ref[:, j * LANES : (j + 1) * LANES]
    order = scatter_order(sta, band)
    here = (lax.axis_index("sta"), lax.axis_index("band"))
    at = 0
    for out in outs:
        for n in range(out.shape[0] // (nrows * per)):
            first = station_of(order[at], here, band, nrows)
            at += 1
            for r in range(nrows):
                source = pl.multiple_of(place[first + r] * per, per)
                to = (n * nrows + r) * per
                out[to : to + per, :] = blocked[pl.ds(source, per), :] * scale


def tile_kernel(
    geometry, n_held, n_out, step, forward, backward, tiles, place, *refs
):
    held, refs = refs[:n_held], refs[n_held:]
    tile, half = None, None
    (th, tl, bc, bs), refs = refs[:4], refs[4:]
    per = geometry[3]
    half = th.shape[0] // 2
    lags = th.shape[1]
    if backward:
        seen, refs = refs[0], refs[1:]
        if not forward:
            given, refs = refs[0], refs[1:]
        outs, refs = refs[:n_out], refs[n_out:]
    else:
        lagged_out, refs = refs[0], refs[1:]
    blocked, ua, ub, rows, cols = refs[:5]
    xh, xl, spec = refs[5:7], refs[7:9], refs[9:11]
    tile = ua.shape[0]
    if backward:
        (folded,) = refs[11:]
    place_stations(held, place, blocked, geometry)
    load_block(blocked, tiles[0, 0], ua, tile, per)
    load_block(blocked, tiles[0, 1], ub, tile, per)
    if backward:
        cols[...] = jnp.zeros_like(cols)

    steps = tile // step
    chunks = half // LANES

    def cross_step(i, c):
        if forward and i < steps:
            cross_rows(c, i * step, step, ua, ub, xh[i % 2], xl[i % 2], tile, half)

    def weigh_step(i, lagged):
        span = slice(i * step * tile, (i + 1) * step * tile)
        if backward:
            misfit = lagged - seen[i * step : (i + 1) * step].reshape(step * tile, lags)
            weighted = misfit + cubic_weight * misfit * misfit * misfit
            folded[span, :] = jnp.concatenate(fold(weighted, lags // 2), 1)
        else:
            lagged_out[span, :] = lagged

    def spectral_step(i, c):
        if i < steps:
            span = slice(i * step * tile, (i + 1) * step * tile)
            at, value = spectral_part(c, chunks, folded, span, bc, bs, lags // 2)
            spec[i % 2][:, at] = value

    cross_step(0, range(chunks))
    for i in range(steps):
        if forward:
            lagged = None
            for c in range(chunks):
                part = lag_part(c, xh[i % 2], xl[i % 2], th, tl, half)
                lagged = part if lagged is None else lagged + part
                cross_step(i + 1, [c])
        else:
            lagged = given[i * step * tile : (i + 1) * step * tile, :]
        weigh_step(i, lagged)
    if backward:
        for c in range(chunks):
            spectral_step(0, c)
        for i in range(steps):
            for c in range(chunks):
                spectral_step(i + 1, c)
                adjoint_rows([c], i * step, step, spec[i % 2], ua, ub, rows, cols, tile, half)
    if backward:
        give_terms(tiles, place, rows, cols, blocked, outs, geometry, tile)


def tile_call(geometry, tiles, place, held, tables, seen, lagged=None, forward=True, backward=True):
    sta, band, rows, per = geometry
    tile, lags = seen.shape[1:]
    width = per * LANES
    step = 24
    count = place.shape[0]
    smem = pl.BlockSpec(memory_space=pltpu.SMEM)
    vmem = pl.BlockSpec(memory_space=pltpu.VMEM)
    args = [tiles, place, *held, *tables]
    specs = [smem] * 2 + [vmem] * (len(held) + 4)
    n_out = 2 if band > 1 else 1
    scratch = [
        pltpu.VMEM((count * per, LANES), f32),
        pltpu.VMEM((tile, width), f32),
        pltpu.VMEM((tile, width), f32),
        pltpu.VMEM((tile, width), f32),
        pltpu.VMEM((tile, width), f32),
    ]
    scratch += [pltpu.VMEM((step * tile, width), bf16)] * 4
    scratch += [pltpu.VMEM((step * tile, width), f32)] * 2
    if backward:
        args.append(seen)
        specs.append(vmem)
        if not forward:
            args.append(lagged)
            specs.append(vmem)
        out_shape = [jax.ShapeDtypeStruct((count * per // n_out, LANES), f32)] * n_out
        scratch += [
            pltpu.VMEM((tile * tile, 5 * (lags // 2)), bf16),
        ]
    else:
        out_shape = [jax.ShapeDtypeStruct((tile * tile, lags), f32)]
    pairs_count = tile * tile
    return pl.pallas_call(
        functools.partial(tile_kernel, geometry, len(held), n_out, step, forward, backward),
        in_specs=specs,
        out_specs=[vmem] * len(out_shape),
        out_shape=out_shape,
        scratch_shapes=scratch,
        compiler_params=pltpu.CompilerParams(vmem_limit_bytes=32 * 2**20),
        cost_estimate=pl.CostEstimate(
            flops=12 * pairs_count * width * lags, bytes_accessed=16 * pairs_count * lags, transcendentals=0
        ),
    )(*args)


def local(sizes, spectra, place, tiles, observed):
    sta, band, src = sizes
    width = spectra.shape[2]
    rows = spectra.shape[1]
    per = width // LANES
    geometry = (sta, band, rows, per)
    piece = spectra.reshape(rows * per, LANES)
    tables = split_table(width // 2, observed.shape[3])
    (own, seen, *tables), (tiles, place) = stage([piece, observed[0], *tables], [tiles, place])
    held = gather(piece, own, sta, band)
    *tables, move = tables
    seen = turn(seen, move, held[0])
    if src == 1:
        parts = tile_call(geometry, tiles, place, held, tables, seen)
    else:
        (lagged,) = tile_call(geometry, tiles, place, held, tables, seen, backward=False)
        lagged = lax.psum(lagged, "src")
        parts = tile_call(geometry, tiles, place, held, tables, seen, lagged, forward=False)
    return scatter_sum(parts, sta, band).reshape(spectra.shape)


def solution(mesh):
    placed = (
        P("src", ("grp", "sta", "band"), None),
        P("grp"),
        P(("grp", "sta", "band"), None),
        P(("grp", "sta", "band"), None, None, None),
    )
    sizes = tuple(mesh.shape[name] for name in ("sta", "band", "src"))
    return jax.shard_map(
        functools.partial(local, sizes),
        mesh=mesh,
        in_specs=placed,
        out_specs=P("src", ("grp", "sta", "band"), None),
        check_vma=False,
    )
```

```python
import functools
import math

import jax
import jax.numpy as jnp
import ml_dtypes
import numpy as np
from jax import lax
from jax.experimental import pallas as pl
from jax.experimental.pallas import tpu as pltpu
from jax.sharding import PartitionSpec as P

cubic_weight = 0.1
LANES = 128
bf16 = jnp.bfloat16
f32 = jnp.float32


def dft_table(freqs, lags):
    fvals = np.arange(freqs, dtype=np.float32)
    tvals = np.arange(lags, dtype=np.float32) - np.float32(lags // 2)
    phase = (np.float32(math.pi / freqs) * fvals[:, None]) * tvals[None, :]
    wave = np.exp(1j * phase.astype(np.float64))
    parts = np.concatenate([wave.real, -wave.imag], 0).astype(np.float32)
    return parts * np.float32(1.0 / math.sqrt(freqs))


def halves(table):
    hi = table.astype(ml_dtypes.bfloat16)
    return hi, (table - hi.astype(np.float32)).astype(ml_dtypes.bfloat16)


def turned(lags):
    return np.concatenate([[0], np.arange(lags // 2 - 1, 0, -1)])


def split_table(freqs, lags):
    table = dft_table(freqs, lags)
    mid = lags // 2
    th, tl = halves(table[:, np.concatenate([np.arange(mid, lags), turned(lags)])])
    even, odd = table[:freqs, mid:].T, table[freqs:, mid:].T.copy()
    odd[0] = table[freqs:, 0]
    ch, cl = halves(even)
    sh, sl = halves(odd)
    eh, el = halves(table[:freqs, 0])
    rest = np.zeros((mid, freqs), ml_dtypes.bfloat16)
    rest[0], rest[1], rest[2] = eh, eh, el
    back = [np.concatenate([ch, ch, cl, rest], 0), np.concatenate([sh, sh, sl], 0)]
    move = np.zeros((mid, mid), ml_dtypes.bfloat16)
    move[turned(lags), np.arange(mid)] = 1
    return [jnp.asarray(t) for t in (th, tl, *back, np.concatenate([move] * 3, 0))]


def split(x):
    hi = x.astype(bf16)
    return hi, (x - hi.astype(f32)).astype(bf16)


def dot(a, b):
    return jnp.dot(a, b, preferred_element_type=f32)


def stage_kernel(*refs):
    count = len(refs) // 2
    sources, (*kept, sems) = refs[:count], refs[count:]
    copies = [pltpu.make_async_copy(s, k, sems.at[n]) for n, (s, k) in enumerate(zip(sources, kept))]
    for copy in copies:
        copy.start()
    for copy in copies:
        copy.wait()


def stage(vectors, scalars):
    arrays = list(vectors) + list(scalars)
    shapes = [pltpu.VMEM(a.shape, a.dtype) for a in vectors]
    shapes += [pltpu.SMEM(a.shape, a.dtype) for a in scalars]
    kept = pl.pallas_call(
        stage_kernel,
        in_specs=[pl.BlockSpec(memory_space=pl.ANY)] * len(arrays),
        out_specs=[pl.BlockSpec(memory_space=pltpu.VMEM)] * len(vectors)
        + [pl.BlockSpec(memory_space=pltpu.SMEM)] * len(scalars),
        out_shape=shapes,
        scratch_shapes=[pltpu.SemaphoreType.DMA((len(arrays),))],
        compiler_params=pltpu.CompilerParams(vmem_limit_bytes=58 * 2**20),
        cost_estimate=pl.CostEstimate(
            flops=0, bytes_accessed=2 * sum(a.size * a.dtype.itemsize for a in vectors), transcendentals=0
        ),
    )(*arrays)
    return kept[: len(vectors)], kept[len(vectors) :]


def turn_kernel(seen, move, after, out):
    rows, pairs_in, lags = seen.shape
    mid = lags // 2
    out[:, :, :mid] = seen[:, :, mid:]
    count = 8
    for p in range(0, rows, count):
        low = seen[p : p + count, :, :mid].reshape(count * pairs_in, mid)
        high, rest = low.astype(bf16), low - low.astype(bf16).astype(f32)
        parts = jnp.concatenate([high, *split(rest)], 1)
        out[p : p + count, :, mid:] = dot(parts, move[...]).reshape(count, pairs_in, mid)


def turn(seen, move, after):
    vmem = pl.BlockSpec(memory_space=pltpu.VMEM)
    return pl.pallas_call(
        turn_kernel,
        in_specs=[vmem, vmem, pl.BlockSpec(memory_space=pl.ANY)],
        out_specs=vmem,
        out_shape=pltpu.VMEM(seen.shape, seen.dtype),
        compiler_params=pltpu.CompilerParams(vmem_limit_bytes=32 * 2**20),
        cost_estimate=pl.CostEstimate(
            flops=3 * seen.size * seen.shape[2], bytes_accessed=8 * seen.size, transcendentals=0
        ),
    )(seen, move, after)


def bits_of(n):
    return [1 << k for k in range(n.bit_length() - 1)]


def gather_order(sta, band):
    order = [(k, 0) for k in range(sta)]
    for bit in reversed(bits_of(band)):
        order = order + [(k, b ^ bit) for k, b in order]
    return order


def scatter_order(sta, band):
    bits = bits_of(band)
    inner = [0]
    for bit in bits[1:]:
        inner = inner + [b ^ bit for b in inner]
    order = [(k, b) for k in range(sta) for b in inner]
    for bit in bits[:1]:
        order = order + [(k, b ^ bit) for k, b in order]
    return order


def pairs(n, k):
    return [(i, i ^ k) for i in range(n)]


def gather(piece, own, sta, band):
    got = {k: lax.ppermute(piece, "sta", pairs(sta, k)) for k in range(sta - 1, 0, -1)}
    held = [jnp.concatenate([own] + [got[k] for k in range(1, sta)], 0)]
    for bit in reversed(bits_of(band)):
        held = held + [lax.ppermute(one, "band", pairs(band, bit)) for one in held]
    return held


def scatter_sum(parts, sta, band):
    bits = bits_of(band)
    total = parts[0]
    if bits:
        total = total + lax.ppermute(parts[1], "band", pairs(band, bits[0]))
    if sta > 1:
        each = total.shape[0] // sta
        sent = [
            lax.ppermute(total[k * each : (k + 1) * each], "sta", pairs(sta, k))
            for k in range(1, sta)
        ]
        total = total[:each]
        for part in reversed(sent):
            total = total + part
    for bit in reversed(bits[1:]):
        half = total.shape[0] // 2
        total = total[:half] + lax.ppermute(total[half:], "band", pairs(band, bit))
    return total


def station_of(offset, me, band, rows):
    return ((offset[0] ^ me[0]) * band + (offset[1] ^ me[1])) * rows


def place_stations(held, place, blocked, geometry):
    sta, band, rows, per = geometry
    order = gather_order(sta, band)
    here = (lax.axis_index("sta"), lax.axis_index("band"))
    at = 0
    for ref in held:
        for n in range(ref.shape[0] // (rows * per)):
            first = station_of(order[at], here, band, rows)
            at += 1
            for r in range(rows):
                to = pl.multiple_of(place[first + r] * per, per)
                blocked[pl.ds(to, per), :] = ref[(n * rows + r) * per : (n * rows + r + 1) * per, :]


def load_block(blocked, block, out, tile, per):
    view = blocked.at[pl.ds(pl.multiple_of(block * (tile * per), tile * per), tile * per)]
    for j in range(per):
        out[:, j * LANES : (j + 1) * LANES] = view[pl.ds(j, tile, stride=per), :]


def cross_rows(chunks, p0, count, ua, ub, xh, xl, tile, half):
    for c in chunks:
        re = slice(c * LANES, (c + 1) * LANES)
        im = slice(half + c * LANES, half + (c + 1) * LANES)
        bre, bim = ub[:, re], ub[:, im]
        ares, aims = ua[p0 : p0 + count, re], ua[p0 : p0 + count, im]
        for p in range(count):
            at = slice(p * tile, (p + 1) * tile)
            are, aim = ares[p : p + 1], aims[p : p + 1]
            xh[at, re], xl[at, re] = split(are * bre + aim * bim)
            xh[at, im], xl[at, im] = split(aim * bre - are * bim)


def lag_part(c, xh, xl, th, tl, half):
    re = slice(c * LANES, (c + 1) * LANES)
    im = slice(half + c * LANES, half + (c + 1) * LANES)
    left = [x[:, at] for x in (xh, xl, xh) for at in (re, im)]
    right = [t[at, :] for t in (th, th, tl) for at in (re, im)]
    return dot(jnp.concatenate(left, 1), jnp.concatenate(right, 0))


def fold(weighted, mid):
    up, down = weighted[:, :mid], weighted[:, mid:]
    column = lax.broadcasted_iota(jnp.int32, up.shape, 1)
    even = jnp.where(column == 0, up, up + down)
    odd = jnp.where(column == 0, down, up - down)
    lone = jnp.broadcast_to(down[:, :1], down.shape)
    high = lone.astype(bf16).astype(f32)
    lone = jnp.where(column == 1, lone - high, high).astype(bf16)
    return (*split(even), lone, *split(odd))


def spectral_part(c, chunks, folded, span, bc, bs, mid):
    size = 2 * LANES
    eh, el, lone, oh, ol = [folded[span, k * mid : (k + 1) * mid] for k in range(5)]
    if c < chunks // 2:
        left, right, here = [eh, el, eh, lone], bc, c
    else:
        left, right, here = [oh, ol, oh], bs, c - chunks // 2
    value = dot(jnp.concatenate(left, 1), right[:, here * size : (here + 1) * size])
    return slice(c * size, (c + 1) * size), value


def adjoint_rows(chunks, p0, count, spec, ua, ub, rows, cols, tile, half):
    for c in chunks:
        re = slice(c * LANES, (c + 1) * LANES)
        im = slice(half + c * LANES, half + (c + 1) * LANES)
        bre, bim = ub[:, re], ub[:, im]
        ares, aims = ua[p0 : p0 + count, re], ua[p0 : p0 + count, im]
        cre, cim = cols[:, re], cols[:, im]
        rre, rim = [], []
        for p in range(count):
            at = slice(p * tile, (p + 1) * tile)
            are, aim = ares[p : p + 1], aims[p : p + 1]
            sre, sim = spec[at, re], spec[at, im]
            rre.append(jnp.sum(sre * bre - sim * bim, axis=0, keepdims=True))
            rim.append(jnp.sum(sre * bim + sim * bre, axis=0, keepdims=True))
            cre = cre + (sre * are + sim * aim)
            cim = cim + (sre * aim - sim * are)
        cols[:, re] = cre
        cols[:, im] = cim
        rows[p0 : p0 + count, re] = jnp.concatenate(rre, 0)
        rows[p0 : p0 + count, im] = jnp.concatenate(rim, 0)


def give_terms(tiles, place, rows, cols, blocked, outs, geometry, tile):
    sta, band, nrows, per = geometry
    scale = 1.0 / tile
    blocked[...] = jnp.zeros_like(blocked)
    for block, ref in ((tiles[0, 0], rows), (tiles[0, 1], cols)):
        view = blocked.at[pl.ds(pl.multiple_of(block * (tile * per), tile * per), tile * per)]
        for j in range(per):
            spot = pl.ds(j, tile, stride=per)
            view[spot, :] = view[spot, :] + ref[:, j * LANES : (j + 1) * LANES]
    order = scatter_order(sta, band)
    here = (lax.axis_index("sta"), lax.axis_index("band"))
    at = 0
    for out in outs:
        for n in range(out.shape[0] // (nrows * per)):
            first = station_of(order[at], here, band, nrows)
            at += 1
            for r in range(nrows):
                source = pl.multiple_of(place[first + r] * per, per)
                to = (n * nrows + r) * per
                out[to : to + per, :] = blocked[pl.ds(source, per), :] * scale


def tile_kernel(
    geometry, n_held, n_out, step, forward, backward, tiles, place, *refs
):
    held, refs = refs[:n_held], refs[n_held:]
    tile, half = None, None
    (th, tl, bc, bs), refs = refs[:4], refs[4:]
    per = geometry[3]
    half = th.shape[0] // 2
    lags = th.shape[1]
    if backward:
        seen, refs = refs[0], refs[1:]
        if not forward:
            given, refs = refs[0], refs[1:]
        outs, refs = refs[:n_out], refs[n_out:]
    else:
        lagged_out, refs = refs[0], refs[1:]
    blocked, ua, ub, rows, cols = refs[:5]
    xh, xl, spec = refs[5:7], refs[7:9], refs[9:11]
    tile = ua.shape[0]
    if backward:
        (folded,) = refs[11:]
    place_stations(held, place, blocked, geometry)
    load_block(blocked, tiles[0, 0], ua, tile, per)
    load_block(blocked, tiles[0, 1], ub, tile, per)
    if backward:
        cols[...] = jnp.zeros_like(cols)

    steps = tile // step
    chunks = half // LANES

    def cross_step(i, c):
        if forward and i < steps:
            cross_rows(c, i * step, step, ua, ub, xh[i % 2], xl[i % 2], tile, half)

    def weigh_step(i, lagged):
        span = slice(i * step * tile, (i + 1) * step * tile)
        if backward:
            misfit = lagged - seen[i * step : (i + 1) * step].reshape(step * tile, lags)
            weighted = misfit + cubic_weight * misfit * misfit * misfit
            folded[span, :] = jnp.concatenate(fold(weighted, lags // 2), 1)
        else:
            lagged_out[span, :] = lagged

    def spectral_step(i, c):
        if i < steps:
            span = slice(i * step * tile, (i + 1) * step * tile)
            at, value = spectral_part(c, chunks, folded, span, bc, bs, lags // 2)
            spec[i % 2][:, at] = value

    cross_step(0, range(chunks))
    for i in range(steps):
        if forward:
            lagged = None
            for c in range(chunks):
                part = lag_part(c, xh[i % 2], xl[i % 2], th, tl, half)
                lagged = part if lagged is None else lagged + part
                cross_step(i + 1, [c])
        else:
            lagged = given[i * step * tile : (i + 1) * step * tile, :]
        weigh_step(i, lagged)
    if backward:
        for c in range(chunks):
            spectral_step(0, c)
        for i in range(steps):
            for c in range(chunks):
                spectral_step(i + 1, c)
                adjoint_rows([c], i * step, step, spec[i % 2], ua, ub, rows, cols, tile, half)
    if backward:
        give_terms(tiles, place, rows, cols, blocked, outs, geometry, tile)


def tile_call(geometry, tiles, place, held, tables, seen, lagged=None, forward=True, backward=True):
    sta, band, rows, per = geometry
    tile, lags = seen.shape[1:]
    width = per * LANES
    step = 24
    count = place.shape[0]
    smem = pl.BlockSpec(memory_space=pltpu.SMEM)
    vmem = pl.BlockSpec(memory_space=pltpu.VMEM)
    args = [tiles, place, *held, *tables]
    specs = [smem] * 2 + [vmem] * (len(held) + 4)
    n_out = 2 if band > 1 else 1
    scratch = [
        pltpu.VMEM((count * per, LANES), f32),
        pltpu.VMEM((tile, width), f32),
        pltpu.VMEM((tile, width), f32),
        pltpu.VMEM((tile, width), f32),
        pltpu.VMEM((tile, width), f32),
    ]
    scratch += [pltpu.VMEM((step * tile, width), bf16)] * 4
    scratch += [pltpu.VMEM((step * tile, width), f32)] * 2
    if backward:
        args.append(seen)
        specs.append(vmem)
        if not forward:
            args.append(lagged)
            specs.append(vmem)
        out_shape = [jax.ShapeDtypeStruct((count * per // n_out, LANES), f32)] * n_out
        scratch += [
            pltpu.VMEM((tile * tile, 5 * (lags // 2)), bf16),
        ]
    else:
        out_shape = [jax.ShapeDtypeStruct((tile * tile, lags), f32)]
    pairs_count = tile * tile
    return pl.pallas_call(
        functools.partial(tile_kernel, geometry, len(held), n_out, step, forward, backward),
        in_specs=specs,
        out_specs=[vmem] * len(out_shape),
        out_shape=out_shape,
        scratch_shapes=scratch,
        compiler_params=pltpu.CompilerParams(vmem_limit_bytes=32 * 2**20),
        cost_estimate=pl.CostEstimate(
            flops=12 * pairs_count * width * lags, bytes_accessed=16 * pairs_count * lags, transcendentals=0
        ),
    )(*args)


def local(sizes, spectra, place, tiles, observed):
    sta, band, src = sizes
    width = spectra.shape[2]
    rows = spectra.shape[1]
    per = width // LANES
    geometry = (sta, band, rows, per)
    piece = spectra.reshape(rows * per, LANES)
    tables = split_table(width // 2, observed.shape[3])
    (own, seen, *tables), (tiles, place) = stage([piece, observed[0], *tables], [tiles, place])
    held = gather(piece, own, sta, band)
    *tables, move = tables
    seen = turn(seen, move, held[0])
    if src == 1:
        parts = tile_call(geometry, tiles, place, held, tables, seen)
    else:
        (lagged,) = tile_call(geometry, tiles, place, held, tables, seen, backward=False)
        lagged = lax.psum(lagged, "src")
        parts = tile_call(geometry, tiles, place, held, tables, seen, lagged, forward=False)
    return scatter_sum(parts, sta, band).reshape(spectra.shape)


def solution(mesh):
    placed = (
        P("src", ("grp", "sta", "band"), None),
        P("grp"),
        P(("grp", "sta", "band"), None),
        P(("grp", "sta", "band"), None, None, None),
    )
    sizes = tuple(mesh.shape[name] for name in ("sta", "band", "src"))
    return jax.shard_map(
        functools.partial(local, sizes),
        mesh=mesh,
        in_specs=placed,
        out_specs=P("src", ("grp", "sta", "band"), None),
        check_vma=False,
    )
```
